32 devices in a mesh: sec: 8 (over z, y), slab: 4 (over x, core).
Axes of the slice: x: 2, y: 2, z: 4, core: 2. Of those that a mesh axis runs over, the one named last changes fastest.
Arguments:
- basis: bfloat16 [16, 1024, 1024], P('sec'), may hold values from -0.1875 to 0.1875
- fermion: bfloat16 [3, 16, 1024, 1024], P(None, 'sec', None, 'slab'), may hold values from -6 to 6
- partner: int32 [3, 16], P(None, 'sec'), may hold values from 0 to 15, as said below
Outputs:
- rotated: bfloat16 [3, 16, 1024, 1024], P(None, 'sec', 'slab')
The draws below stay inside these ranges and needn't reach their ends.
Inputs may be any that keep to these rules, and one draw needn't show every extreme that they name: partner[f, Q] // 2 equals Q // 2 or (Q // 2 + 1) % 8, so a partner lies in the block of 2 sectors that holds Q or in the next block, the last block's next being the first.
All inputs are finite; a program needn't handle non-finite values.
Results may differ from the reference program's by a relative error of at most 0.0049.
Values may be sent and summed in bfloat16 or wider, within the bound.
No kernel may reach another device: no remote copies, remote signals or barrier semaphores. Data moves between devices by JAX's collectives and lax.ppermute only.
A program may use at most 64 MiB of HBM per device.

```python
import jax
import jax.numpy as jnp
from jax import lax

NB = 1024
FL = 3
SEC_DEV = 2
S = 16


def draw_partner(key, part):
    offset = jax.random.randint(key, (FL, S), 1, SEC_DEV + 1)
    sector_ids = jnp.arange(S, dtype=jnp.int32)[None, :]
    target = sector_ids + offset
    result = jnp.where(target < S, target, 2 * S - 1 - target).astype(jnp.int32)
    result = jnp.where(sector_ids == S - 2, S - 1, result)
    result = jnp.where(sector_ids == S - 1, 0, result)
    return result.astype(jnp.int32)


def shard_levels(rng, extent, cuts, smallest, high):
    def one(axis_at, parts):
        heights = jax.random.uniform(jax.random.fold_in(jax.random.fold_in(rng, 6), axis_at), (parts,), jnp.float32, smallest / len(cuts), high / len(cuts))
        return jnp.repeat(jnp.exp(heights), extent[axis_at] // parts).reshape((-1,) + (1,) * (len(extent) - axis_at - 1))

    level = one(*cuts[0])
    for cut in cuts[1:]:
        level = level * one(*cut)
    return level


def normal_values(own_key, dims, deviation, most, pieces=(), kind=jnp.bfloat16):
    drawn = deviation * jax.random.normal(own_key, dims, jnp.float32)
    if pieces:
        drawn = drawn * shard_levels(own_key, dims, pieces, -0.22, 0.18)
    return jnp.clip(drawn, -most, most).astype(kind)


def setup_inputs(seed: int = 0) -> dict:
    key_of = jax.random.split(jax.random.key(seed), 4)
    return {
        "basis": normal_values(key_of[0], (S, NB, NB), NB ** -0.5, 0.1875, ((0, 8),)),
        "fermion": normal_values(key_of[1], (FL, S, NB, NB), 1.0, 6.0, ((1, 8), (3, 4))),
        "partner": draw_partner(jax.random.fold_in(key_of[3], 71), 0),
    }


def reference(basis, fermion, partner):
    def sector(index):
        left_basis = basis[index]
        blocks = []
        for flavour in range(FL):
            half_rotated = jnp.dot(left_basis.T, fermion[flavour, index], preferred_element_type=jnp.float32).astype(jnp.bfloat16)
            right_basis = basis[partner[flavour, index]]
            blocks.append(jnp.dot(half_rotated, right_basis, preferred_element_type=jnp.float32).astype(jnp.bfloat16))
        return jnp.stack(blocks)

    rotated = lax.map(sector, jnp.arange(S, dtype=jnp.int32))
    return jnp.transpose(rotated, (1, 0, 2, 3))
```

```python
import functools

import jax
import jax.numpy as jnp
from jax import lax
from jax.experimental import pallas as pl
from jax.experimental.pallas import tpu as pltpu
from jax.sharding import PartitionSpec as P

ANY = pl.BlockSpec(memory_space=pl.ANY)
SCALAR = pl.BlockSpec(memory_space=pltpu.SMEM)
WHOLE = pl.BlockSpec(memory_space=pltpu.VMEM)
OWN, OTHER = -1, -2
KERNEL_BYTES = 14 * 1024 * 1024
LONG = pl.CostEstimate(flops=10**12, bytes_accessed=0, transcendentals=0)
BRIEF = pl.CostEstimate(flops=0, bytes_accessed=0, transcendentals=0)


def in_hbm(array):
    return pltpu.with_memory_space_constraint(array, pltpu.HBM)


def in_vmem(array):
    return pltpu.with_memory_space_constraint(array, pltpu.VMEM)


def first_column(start, columns, place):
    if start == OWN:
        return pl.multiple_of(place[3] + (place[0] // 2) * columns, columns)
    if start == OTHER:
        return pl.multiple_of(place[3] + (1 - place[0] // 2) * columns, columns)
    return start


def previous(block):
    count = lax.axis_size("sec")
    return lax.ppermute(block, "sec", [((i + 1) % count, i) for i in range(count)])


def swapped(block, distance):
    return lax.ppermute(block, "slab", [(i, i ^ distance) for i in range(lax.axis_size("slab"))])


def send_copies(parts, place, basis, sent, sems):
    width = basis.shape[1] // lax.axis_size("slab")
    here = place[0]
    copies = []
    for at, spans in enumerate(parts):
        column = 0
        for start, columns in spans:
            start = first_column(start, columns, place)
            for block in range(basis.shape[1] // width // 2):
                row = pl.multiple_of((2 * block + here % 2) * width, width)
                copies.append(
                    pltpu.make_async_copy(
                        basis.at[:, pl.ds(row, width), pl.ds(start, columns)],
                        sent[at].at[:, pl.ds(block * width, width), pl.ds(column, columns)],
                        sems.at[len(copies)],
                    )
                )
            column += columns
    return copies


def half_products(distances, place, basis, fermion, pieces, ready):
    flavours, sectors, _, width = fermion.shape
    for sector in range(sectors):
        ready(sector)
        right = jnp.concatenate([fermion[flavour, sector] for flavour in range(flavours)], axis=1)
        for slot, distance in enumerate(distances):
            column = pl.multiple_of((place[0] ^ distance) * width, width)
            block = lax.dot_general(
                basis[sector, :, pl.ds(column, width)],
                right,
                (((0,), (0,)), ((), ())),
                preferred_element_type=jnp.float32,
            ).astype(jnp.bfloat16)
            for flavour in range(flavours):
                pieces[slot][sector, flavour] = block[:, flavour * width : (flavour + 1) * width]


def first_kernel(parts, distances, place, basis, fermion, *refs):
    sent, refs = refs[: len(parts)], refs[len(parts) :]
    *pieces, left, right, sems, left_sems, right_sems = refs
    flavours, sectors, _, width = fermion.shape
    sent_copies = send_copies(parts, place, basis, sent, sems)
    for copy in sent_copies:
        copy.start()

    @pl.when(place[1] == 0)
    def _():
        copies = []
        for sector in range(sectors):
            copies.append([pltpu.make_async_copy(basis.at[sector], left.at[sector], left_sems.at[sector])])
            for flavour in range(flavours):
                copies[-1].append(
                    pltpu.make_async_copy(
                        fermion.at[flavour, sector], right.at[flavour, sector], right_sems.at[sector, flavour]
                    )
                )
        for group in copies:
            for copy in group:
                copy.start()

        def ready(sector):
            for copy in copies[sector]:
                copy.wait()

        half_products(distances, place, left, right, pieces, ready)

    for copy in sent_copies:
        copy.wait()


def first_call(place, basis, fermion, parts, distances):
    flavours, sectors, depth, width = fermion.shape
    copies = sum(len(spans) for spans in parts) * lax.axis_size("slab") // 2
    return pl.pallas_call(
        functools.partial(first_kernel, parts, distances),
        out_shape=[
            pltpu.VMEM((sectors, depth // 2, sum(columns for _, columns in spans)), jnp.bfloat16) for spans in parts
        ]
        + [pltpu.VMEM((sectors, flavours, width, width), jnp.bfloat16)] * len(distances),
        in_specs=[SCALAR, ANY, ANY],
        out_specs=[WHOLE] * (len(parts) + len(distances)),
        scratch_shapes=[
            pltpu.VMEM((sectors, depth, depth), jnp.bfloat16),
            pltpu.VMEM((flavours, sectors, depth, width), jnp.bfloat16),
            pltpu.SemaphoreType.DMA((copies,)),
            pltpu.SemaphoreType.DMA((sectors,)),
            pltpu.SemaphoreType.DMA((sectors, flavours)),
        ],
        compiler_params=pltpu.CompilerParams(vmem_limit_bytes=KERNEL_BYTES),
        cost_estimate=BRIEF,
        name="first",
    )(place, in_hbm(basis), in_hbm(fermion))


def other_half_kernel(distances, place, basis, fermion, *refs):
    @pl.when(place[1] != 0)
    def _():
        half_products(distances, place, basis, fermion, refs[len(distances) :], lambda sector: None)


def half_blocks(place, basis, fermion, distances, earlier):
    flavours, sectors, depth, width = fermion.shape
    return pl.pallas_call(
        functools.partial(other_half_kernel, distances),
        out_shape=[pltpu.VMEM((sectors, flavours, width, width), jnp.bfloat16)] * len(distances),
        in_specs=[SCALAR] + [WHOLE] * (2 + len(earlier)),
        out_specs=[WHOLE] * len(distances),
        input_output_aliases={3 + i: i for i in range(len(earlier))},
        compiler_params=pltpu.CompilerParams(vmem_limit_bytes=KERNEL_BYTES),
        cost_estimate=BRIEF,
        name="half",
    )(place, *map(in_vmem, (basis, fermion, *earlier)))


def cut_kernel(cuts, given, *refs):
    for cut, piece in zip(cuts, refs[-len(cuts) :]):
        piece[...] = given[cut]


def cut_out(array, cuts, after=()):
    shapes = [jax.eval_shape(lambda x, cut=cut: x[cut], array).shape for cut in cuts]
    return pl.pallas_call(
        functools.partial(cut_kernel, cuts),
        out_shape=[pltpu.VMEM(shape, array.dtype) for shape in shapes],
        in_specs=[WHOLE] * (1 + len(after)),
        out_specs=[WHOLE] * len(cuts),
        compiler_params=pltpu.CompilerParams(vmem_limit_bytes=KERNEL_BYTES),
        cost_estimate=BRIEF,
        name="cut",
    )(in_vmem(array), *map(in_vmem, after))


def span_copies(spans, first, place, basis, right, sems):
    sectors = basis.shape[0]
    copies, at = [], 0
    for start, columns in spans:
        copies.append(
            pltpu.make_async_copy(
                basis.at[:, :, pl.ds(first_column(start, columns, place), columns)],
                right.at[pl.ds(0, sectors), :, pl.ds(at, columns)],
                sems.at[first + len(copies)],
            )
        )
        at += columns
    return copies


def next_copies(nexts, first, place, right, sems):
    here = place[0]
    sectors = right.shape[0] // 2
    width = right.shape[1] // lax.axis_size("slab")
    copies, at = [], 0
    for pair in nexts:
        columns = pair[0].shape[2]
        for side in range(2):
            for block in range(right.shape[1] // width // 2):
                row = pl.multiple_of((2 * block + (here + side) % 2) * width, width)
                copies.append(
                    pltpu.make_async_copy(
                        pair[side].at[:, pl.ds(block * width, width)],
                        right.at[pl.ds(sectors, sectors), pl.ds(row, width), pl.ds(at, columns)],
                        sems.at[first + len(copies)],
                    )
                )
        at += columns
    return copies


def multiply(spans, place, partner, left, right, stage, out, sems):
    flavours, sectors = stage.shape[:2]
    copies = []
    for sector in range(sectors):
        for flavour in range(flavours):
            index = (partner[sector, flavour] - place[1] + place[2]) % place[2]
            stage[flavour, sector] = jnp.dot(
                left[sector, flavour], right[index], preferred_element_type=jnp.float32
            ).astype(jnp.bfloat16)
            at = 0
            for start, columns in spans:
                copy = pltpu.make_async_copy(
                    stage.at[flavour, sector, :, pl.ds(at, columns)],
                    out.at[flavour, sector, :, pl.ds(first_column(start, columns, place), columns)],
                    sems.at[len(copies)],
                )
                copy.start()
                copies.append(copy)
                at += columns
    for copy in copies:
        copy.wait()


def early_kernel(spans, pairs, distances, place, partner, basis, *refs):
    halves, refs = refs[: len(distances)], refs[len(distances) :]
    nexts, refs = [refs[2 * i : 2 * i + 2] for i in range(pairs)], refs[2 * pairs :]
    out, left, right, stage, in_sems, out_sems = refs
    width = stage.shape[2]
    copies = span_copies(spans, 0, place, basis, right, in_sems)
    copies += next_copies(nexts, len(copies), place, right, in_sems)
    for half, (sector, many, distance) in zip(halves, distances):
        column = pl.multiple_of((place[0] ^ distance) * width, width)
        copies.append(
            pltpu.make_async_copy(
                half, left.at[pl.ds(sector, many), :, :, pl.ds(column, width)], in_sems.at[len(copies)]
            )
        )
    for copy in copies:
        copy.start()
    for copy in copies:
        copy.wait()
    multiply(spans, place, partner, left, right, stage, out, out_sems)


def late_kernel(spans, pairs, place, partner, basis, *refs):
    nexts, refs = [refs[2 * i : 2 * i + 2] for i in range(pairs)], refs[2 * pairs :]
    left, _, out, right, stage, in_sems, out_sems = refs
    copies = span_copies(spans, 0, place, basis, right, in_sems)
    copies += next_copies(nexts, len(copies), place, right, in_sems)
    for copy in copies:
        copy.start()
    for copy in copies:
        copy.wait()
    multiply(spans, place, partner, left, right, stage, out, out_sems)


def early_products(place, partner, basis, spans, nexts, halves, distances):
    sectors, depth, _ = basis.shape
    flavours, width = halves[0].shape[1:3]
    columns = sum(span[1] for span in spans)
    given = [in_vmem(array) for array in (basis, *halves, *(array for pair in nexts for array in pair))]
    copies = len(spans) + len(nexts) * lax.axis_size("slab") + len(halves)
    return pl.pallas_call(
        functools.partial(early_kernel, spans, len(nexts), distances),
        out_shape=[
            pltpu.HBM((flavours, sectors, width, depth), jnp.bfloat16),
            pltpu.VMEM((sectors, flavours, width, depth), jnp.bfloat16),
        ],
        in_specs=[SCALAR, SCALAR] + [WHOLE] * len(given),
        out_specs=[ANY, WHOLE],
        scratch_shapes=[
            pltpu.VMEM((2 * sectors, depth, columns), jnp.bfloat16),
            pltpu.VMEM((flavours, sectors, width, columns), jnp.bfloat16),
            pltpu.SemaphoreType.DMA((copies,)),
            pltpu.SemaphoreType.DMA((flavours * sectors * len(spans),)),
        ],
        compiler_params=pltpu.CompilerParams(vmem_limit_bytes=KERNEL_BYTES),
        cost_estimate=BRIEF,
        name="early",
    )(place, partner, *given)


def late_products(place, partner, basis, spans, nexts, out, left):
    sectors, flavours, width, depth = left.shape
    columns = sum(span[1] for span in spans)
    given = [in_vmem(array) for array in (basis, *(array for pair in nexts for array in pair), left)]
    return pl.pallas_call(
        functools.partial(late_kernel, spans, len(nexts)),
        out_shape=pltpu.HBM(out.shape, out.dtype),
        in_specs=[SCALAR, SCALAR] + [WHOLE] * len(given) + [ANY],
        out_specs=ANY,
        scratch_shapes=[
            pltpu.VMEM((2 * sectors, depth, columns), jnp.bfloat16),
            pltpu.VMEM((flavours, sectors, width, columns), jnp.bfloat16),
            pltpu.SemaphoreType.DMA((len(spans) + len(nexts) * lax.axis_size("slab"),)),
            pltpu.SemaphoreType.DMA((flavours * sectors * len(spans),)),
        ],
        input_output_aliases={2 + len(given): 0},
        compiler_params=pltpu.CompilerParams(vmem_limit_bytes=KERNEL_BYTES),
        cost_estimate=BRIEF,
        name="late",
    )(place, partner, *given, out)


def local(basis, fermion, partner):
    sectors, depth, _ = basis.shape
    every = sectors * lax.axis_size("sec")
    here = lax.axis_index("slab")
    unit = depth // 8
    place = jnp.stack([here, lax.axis_index("sec") * sectors, every, depth - 2 * unit]).astype(jnp.int32)
    spans, middle_spans, late_spans = ((0, 3 * unit), (OWN, unit)), ((3 * unit, 3 * unit),), ((OTHER, unit),)
    distances = (0, 1, 2, 3)
    first_part, last_part, *halves = first_call(place, basis, fermion, (spans, middle_spans), distances)
    first, last = previous(first_part), previous(last_part)
    near, mine, far2, far3 = half_blocks(place, basis, fermion, distances, halves)
    got2, got3, beside = swapped(far2, 2), swapped(far3, 3), swapped(mine, 1)
    *rest, own = cut_out(
        first,
        [(slice(None), slice(None), slice(at * unit, at * unit + unit)) for at in range(4)],
        (beside, got2),
    )
    shared = swapped(own, 2)
    nexts = [(piece, swapped(piece, 1)) for piece in (*rest, own)]
    blocks = [(0, sectors, distance) for distance in distances[::-1]]
    earlier = early_products(place, partner.T, basis, spans, nexts, [got3, got2, beside, near], blocks)
    shared, last, out = lax.optimization_barrier((shared, last, earlier[0]))
    nexts = [(last, swapped(last, 1)), (shared, swapped(shared, 1))]
    return late_products(place, partner.T, basis, middle_spans + late_spans, nexts, out, earlier[1])


def solution(mesh):
    placed = (P("sec", None, None), P(None, "sec", None, "slab"), P(None, "sec"))
    return jax.shard_map(
        local, mesh=mesh, in_specs=placed, out_specs=P(None, "sec", "slab", None), check_vma=False
    )
```

```python
import functools

import jax
import jax.numpy as jnp
from jax import lax
from jax.experimental import pallas as pl
from jax.experimental.pallas import tpu as pltpu
from jax.sharding import PartitionSpec as P

ANY = pl.BlockSpec(memory_space=pl.ANY)
SCALAR = pl.BlockSpec(memory_space=pltpu.SMEM)
WHOLE = pl.BlockSpec(memory_space=pltpu.VMEM)
OWN, OTHER = -1, -2
KERNEL_BYTES = 16 * 1024 * 1024
BRIEF = pl.CostEstimate(flops=0, bytes_accessed=0, transcendentals=0)


def in_hbm(array):
    return pltpu.with_memory_space_constraint(array, pltpu.HBM)


def in_vmem(array):
    return pltpu.with_memory_space_constraint(array, pltpu.VMEM)


def kernel_call(body, name, given, specs, shapes, out_specs, scratch=(), aliases={}, cost=BRIEF):
    return pl.pallas_call(
        body,
        out_shape=shapes,
        in_specs=specs,
        out_specs=out_specs,
        scratch_shapes=list(scratch),
        input_output_aliases=aliases,
        compiler_params=pltpu.CompilerParams(vmem_limit_bytes=KERNEL_BYTES),
        cost_estimate=cost,
        name=name,
    )(*given)


def first_column(unit, place, width):
    if unit == OWN:
        return pl.multiple_of(place[3] + (place[0] // 2) * width, width)
    if unit == OTHER:
        return pl.multiple_of(place[3] + (1 - place[0] // 2) * width, width)
    return unit * width


def run(copies):
    for copy in copies:
        copy.start()
    for copy in copies:
        copy.wait()


def previous(block):
    count = lax.axis_size("sec")
    return lax.ppermute(block, "sec", [((i + 1) % count, i) for i in range(count)])


def swapped(block, distance):
    return lax.ppermute(block, "slab", [(i, i ^ distance) for i in range(lax.axis_size("slab"))])


def part_kernel(lists, unit, distances, place, basis, fermion, *refs):
    sent, refs = refs[: len(lists)], refs[len(lists) :]
    *pieces, left, right, sems, half_sems = refs
    slabs = lax.axis_size("slab")
    rows = basis.shape[1] // slabs
    copies = []
    for array, blocks in zip(sent, lists):
        for at, (sector, count, start) in enumerate(blocks):
            for slab in range(slabs // 2):
                row = pl.multiple_of((2 * slab + place[0] % 2) * rows, rows)
                copies.append(
                    pltpu.make_async_copy(
                        basis.at[sector, pl.ds(row, rows), pl.ds(first_column(start, place, unit), count * unit)],
                        array.at[at, pl.ds(slab * rows, rows)],
                        sems.at[len(copies)],
                    )
                )
    for copy in copies:
        copy.start()

    @pl.when(place[1] == 0)
    def _():
        run(
            [
                pltpu.make_async_copy(basis.at[pl.ds(0, 1)], left, half_sems.at[0]),
                pltpu.make_async_copy(fermion.at[:, pl.ds(0, 1)], right, half_sems.at[1]),
            ]
        )
        half_products(0, distances, place, left, right, pieces)

    for copy in copies:
        copy.wait()


def basis_parts(place, basis, fermion, lists, unit, distances):
    flavours, sectors, depth, width = fermion.shape
    copies = sum(len(blocks) for blocks in lists) * lax.axis_size("slab") // 2
    shapes = [pltpu.VMEM((len(blocks), depth // 2, blocks[0][1] * unit), jnp.bfloat16) for blocks in lists]
    shapes += [pltpu.VMEM((sectors, flavours, width, width), jnp.bfloat16)] * len(distances)
    return kernel_call(
        functools.partial(part_kernel, lists, unit, distances),
        "part",
        [place, in_hbm(basis), in_hbm(fermion)],
        [SCALAR, ANY, ANY],
        shapes,
        [WHOLE] * len(shapes),
        [
            pltpu.VMEM((1, depth, depth), jnp.bfloat16),
            pltpu.VMEM((flavours, 1, depth, width), jnp.bfloat16),
            pltpu.SemaphoreType.DMA((copies,)),
            pltpu.SemaphoreType.DMA((2,)),
        ],
    )


def half_products(sector, distances, place, basis, fermion, pieces):
    flavours, _, _, width = fermion.shape
    right = jnp.concatenate([fermion[flavour, sector] for flavour in range(flavours)], axis=1)
    for slot, distance in enumerate(distances):
        column = pl.multiple_of((place[0] ^ distance) * width, width)
        block = lax.dot_general(
            basis[sector, :, pl.ds(column, width)],
            right,
            (((0,), (0,)), ((), ())),
            preferred_element_type=jnp.float32,
        ).astype(jnp.bfloat16)
        for flavour in range(flavours):
            pieces[slot][sector, flavour] = block[:, flavour * width : (flavour + 1) * width]


def half_kernel(distances, place, basis, fermion, *refs):
    pieces = refs[len(distances) :]

    @pl.when(place[1] != 0)
    def _():
        half_products(0, distances, place, basis, fermion, pieces)

    for sector in range(1, basis.shape[0]):
        half_products(sector, distances, place, basis, fermion, pieces)


def half_blocks(place, basis, fermion, distances, earlier):
    return kernel_call(
        functools.partial(half_kernel, distances),
        "half",
        [place, in_vmem(basis), in_vmem(fermion), *map(in_vmem, earlier)],
        [SCALAR] + [WHOLE] * (2 + len(earlier)),
        [pltpu.VMEM(piece.shape, piece.dtype) for piece in earlier],
        [WHOLE] * len(distances),
        aliases={3 + at: at for at in range(len(earlier))},
    )


def cut_kernel(cuts, given, *refs):
    for cut, piece in zip(cuts, refs[-len(cuts) :]):
        piece[...] = given[cut]


def cut_out(array, cuts, after=()):
    shapes = [jax.eval_shape(lambda x, cut=cut: x[cut], array).shape for cut in cuts]
    return kernel_call(
        functools.partial(cut_kernel, cuts),
        "cut",
        [in_vmem(array), *map(in_vmem, after)],
        [WHOLE] * (1 + len(after)),
        [pltpu.VMEM(shape, array.dtype) for shape in shapes],
        [WHOLE] * len(cuts),
    )


def own_copies(units, unit, place, basis, right, sems, first):
    sectors, depth, _ = basis.shape
    slabs = lax.axis_size("slab")
    rows = depth // slabs
    copies, at = [], 0
    for start, count in units:
        for slab in range(slabs):
            to = ((slab % 2) * (slabs // 2) + slab // 2) * rows
            copies.append(
                pltpu.make_async_copy(
                    basis.at[:, pl.ds(slab * rows, rows), pl.ds(first_column(start, place, unit), count * unit)],
                    right.at[pl.ds(0, sectors), pl.ds(to, rows), pl.ds(at, count * unit)],
                    sems.at[first + len(copies)],
                )
            )
        at += count * unit
    return copies


def next_copies(nexts, place, pairs, right, sems, first):
    sectors, depth = right.shape[0] // 2, right.shape[1]
    copies = []
    for pair, holds in zip(pairs, nexts):
        for index, many, sector, column in holds:
            for side in range(2):
                to = pl.multiple_of(((place[0] + side) % 2) * (depth // 2), depth // 2)
                copies.append(
                    pltpu.make_async_copy(
                        pair[side].at[pl.ds(index, many)],
                        right.at[
                            pl.ds(sectors + sector, many), pl.ds(to, depth // 2), pl.ds(column, pair[side].shape[2])
                        ],
                        sems.at[first + len(copies)],
                    )
                )
    return copies


def half_copy(half, distance, place, left, sem):
    slabs = lax.axis_size("slab")
    width = half.shape[3]
    slab = place[0] ^ distance
    column = pl.multiple_of(((slab % 2) * (slabs // 2) + slab // 2) * width, width)
    return pltpu.make_async_copy(half, left.at[:, :, :, pl.ds(column, width)], sem)


def gather_kernel(early_units, late_units, nexts, unit, distances, cut, place, basis, *refs):
    halves, refs = refs[: len(distances)], refs[len(distances) :]
    pairs, refs = [refs[2 * i : 2 * i + 2] for i in range(len(nexts))], refs[2 * len(nexts) :]
    left, early_right, late_right, sent, sems = refs
    copies = own_copies(early_units, unit, place, basis, early_right, sems, 0)
    copies += next_copies(nexts, place, pairs, early_right, sems, len(copies))
    copies += own_copies(late_units, unit, place, basis, late_right, sems, len(copies))
    for half, distance in zip(halves, distances):
        copies.append(half_copy(half, distance, place, left, sems.at[len(copies)]))
    copies.append(pltpu.make_async_copy(pairs[-1][0].at[cut], sent, sems.at[len(copies)]))
    run(copies)


def gather(place, basis, early_units, late_units, nexts, unit, pairs, halves, distances, cut):
    sectors, depth, _ = basis.shape
    flavours, width = halves[0].shape[1:3]
    given = [in_vmem(array) for array in (basis, *halves, *(array for pair in pairs for array in pair))]
    early_columns, late_columns = (sum(count for _, count in units) * unit for units in (early_units, late_units))
    copies = (len(early_units) + len(late_units)) * (depth // width) + 2 * sum(len(holds) for holds in nexts)
    last = pairs[-1][0]
    return kernel_call(
        functools.partial(gather_kernel, early_units, late_units, nexts, unit, distances, cut),
        "gather",
        [place, *given],
        [SCALAR] + [WHOLE] * len(given),
        [
            pltpu.VMEM((sectors, flavours, width, depth), jnp.bfloat16),
            pltpu.VMEM((2 * sectors, depth, early_columns), jnp.bfloat16),
            pltpu.VMEM((2 * sectors, depth, late_columns), jnp.bfloat16),
            pltpu.VMEM((cut.size, *last.shape[1:]), jnp.bfloat16),
        ],
        [WHOLE] * 4,
        [pltpu.SemaphoreType.DMA((copies + len(halves) + 1,))],
    )


def product(place, partner, sector, flavour, left, right):
    index = (partner[sector, flavour] - place[1] + place[2]) % place[2]
    return jnp.dot(left[sector, flavour], right[index], preferred_element_type=jnp.float32).astype(jnp.bfloat16)


def early_kernel(distance, place, partner, half, right, _, left, stage, sem):
    run([half_copy(half, distance, place, left, sem)])
    sectors, flavours = left.shape[:2]
    for sector in range(sectors):
        for flavour in range(flavours):
            stage[flavour, sector] = product(place, partner, sector, flavour, left, right)


def early_products(place, partner, half, distance, left, right):
    sectors, flavours, width, _ = left.shape
    return kernel_call(
        functools.partial(early_kernel, distance),
        "early",
        [place, partner, in_vmem(half), in_vmem(right), in_vmem(left)],
        [SCALAR, SCALAR] + [WHOLE] * 3,
        [
            pltpu.VMEM(left.shape, left.dtype),
            pltpu.VMEM((flavours, sectors, width, right.shape[2]), jnp.bfloat16),
        ],
        [WHOLE] * 2,
        [pltpu.SemaphoreType.DMA],
        {4: 0},
    )


def late_kernel(early_units, units, nexts, unit, place, partner, left, early, *refs):
    pairs, refs = [refs[2 * i : 2 * i + 2] for i in range(len(nexts))], refs[2 * len(nexts) :]
    _, out, right, stage, sems, early_sems, out_sems = refs
    sectors, flavours = left.shape[:2]
    next_here = next_copies(nexts, place, pairs, right, sems, 0)
    for copy in next_here:
        copy.start()
    out_copies, at = [], 0
    for start, count in early_units:
        out_copies.append(
            pltpu.make_async_copy(
                early.at[:, :, :, pl.ds(at, count * unit)],
                out.at[:, :, :, pl.ds(first_column(start, place, unit), count * unit)],
                early_sems.at[len(out_copies)],
            )
        )
        out_copies[-1].start()
        at += count * unit
    for copy in next_here:
        copy.wait()
    for sector in range(sectors):
        for flavour in range(flavours):
            stage[flavour, sector] = product(place, partner, sector, flavour, left, right)
            at = 0
            for number, (start, count) in enumerate(units):
                copy = pltpu.make_async_copy(
                    stage.at[flavour, sector, :, pl.ds(at, count * unit)],
                    out.at[flavour, sector, :, pl.ds(first_column(start, place, unit), count * unit)],
                    out_sems.at[sector * flavours + flavour, number],
                )
                copy.start()
                out_copies.append(copy)
                at += count * unit
    for copy in out_copies:
        copy.wait()


def late_products(place, partner, early_units, units, nexts, unit, pairs, left, early, right):
    sectors, flavours, width, depth = left.shape
    given = [in_vmem(array) for array in (left, early, *(array for pair in pairs for array in pair), right)]
    return kernel_call(
        functools.partial(late_kernel, early_units, units, nexts, unit),
        "late",
        [place, partner, *given],
        [SCALAR, SCALAR] + [WHOLE] * len(given),
        [
            pltpu.HBM((flavours, sectors, width, depth), jnp.bfloat16),
            pltpu.VMEM(right.shape, right.dtype),
        ],
        [ANY, WHOLE],
        [
            pltpu.VMEM((flavours, sectors, width, right.shape[2]), jnp.bfloat16),
            pltpu.SemaphoreType.DMA((2 * sum(len(holds) for holds in nexts),)),
            pltpu.SemaphoreType.DMA((len(early_units),)),
            pltpu.SemaphoreType.DMA((sectors * flavours, len(units))),
        ],
        {1 + len(given): 1},
    )[0]


def local(basis, fermion, partner):
    sectors, depth, _ = basis.shape
    every = sectors * lax.axis_size("sec")
    unit = depth // 8
    place = jnp.stack([lax.axis_index("slab"), lax.axis_index("sec") * sectors, every, depth - 2 * unit])
    place = place.astype(jnp.int32)
    partner = partner.T
    distances = (3, 2, 1, 0)
    alone = sectors // 2
    count = 3
    early_units, late_units = ((0, count), (OWN, 1)), ((count, 6 - count), (OTHER, 1))
    first_blocks = [(sector, 1, start) for start in (*range(count), OWN) for sector in range(sectors)]
    last_blocks = [(sector, 1, start) for start in range(count, 6) for sector in range(sectors)]
    last_blocks += [(sector, 1, OTHER) for sector in range(alone)]
    first_part, last_part, *halves = basis_parts(
        place, basis, fermion, (first_blocks, last_blocks), unit, distances
    )
    first, last = previous(first_part), previous(last_part)
    far3, far2, mine, near = half_blocks(place, basis, fermion, distances, halves)
    got2, got3, beside = swapped(far2, 2), swapped(far3, 3), swapped(mine, 1)
    groups = ((0, 2), (2, 4))
    pieces = cut_out(first, [slice(begin * sectors, end * sectors) for begin, end in groups], (beside, got2))
    pairs = [(piece, swapped(piece, 1)) for piece in pieces]
    nexts = [
        [((at - begin) * sectors, sectors, 0, at * unit) for at in range(begin, end)] for begin, end in groups
    ]
    begin, end = groups[-1]
    cut = pl.ds((end - 1 - begin) * sectors + alone, sectors - alone)
    left, early_right, late_right, sent = gather(
        place, basis, early_units, late_units, nexts, unit, pairs, [got2, beside, near], distances[1:], cut
    )
    other = swapped(sent, 2)
    left, early = early_products(place, partner, got3, distances[0], left, early_right)
    nexts = [[(at * sectors, sectors, 0, at * unit) for at in range(6 - count)]]
    if alone:
        nexts[0].append(((6 - count) * sectors, alone, 0, (6 - count) * unit))
    nexts.append([(0, sectors - alone, alone, (6 - count) * unit)])
    last, other, early = lax.optimization_barrier((last, other, early))
    pairs = [(last, swapped(last, 1)), (other, swapped(other, 1))]
    return late_products(place, partner, early_units, late_units, nexts, unit, pairs, left, early, late_right)


def solution(mesh):
    placed = (P("sec", None, None), P(None, "sec", None, "slab"), P(None, "sec"))
    return jax.shard_map(
        local, mesh=mesh, in_specs=placed, out_specs=P(None, "sec", "slab", None), check_vma=False
    )
```

```python
import functools

import jax
import jax.numpy as jnp
from jax import lax
from jax.experimental import pallas as pl
from jax.experimental.pallas import tpu as pltpu
from jax.sharding import PartitionSpec as P

ANY = pl.BlockSpec(memory_space=pl.ANY)
WHOLE = pl.BlockSpec(memory_space=pltpu.VMEM)
OWN, OTHER = -1, -2
KERNEL_BYTES = 16 * 1024 * 1024
BRIEF = pl.CostEstimate(flops=0, bytes_accessed=0, transcendentals=0)


def in_hbm(array):
    return pltpu.with_memory_space_constraint(array, pltpu.HBM)


def in_vmem(array):
    return pltpu.with_memory_space_constraint(array, pltpu.VMEM)


def located(sectors, depth):
    first = lax.axis_index("sec") * sectors
    return lax.axis_index("slab"), first, lax.axis_size("sec") * sectors, depth - depth // 8 * 2


def kernel_call(body, name, shape, given, specs, shapes, out_specs, scratch=(), aliases={}, cost=BRIEF):
    def kernel(*refs):
        body(*(() if shape is None else (located(*shape),)), *refs)

    return pl.pallas_call(
        kernel,
        out_shape=shapes,
        in_specs=specs,
        out_specs=out_specs,
        scratch_shapes=list(scratch),
        input_output_aliases=aliases,
        compiler_params=pltpu.CompilerParams(vmem_limit_bytes=KERNEL_BYTES),
        cost_estimate=cost,
        name=name,
    )(*given)


def first_column(unit, place, width):
    if unit == OWN:
        return pl.multiple_of(place[3] + (place[0] // 2) * width, width)
    if unit == OTHER:
        return pl.multiple_of(place[3] + (1 - place[0] // 2) * width, width)
    return unit * width


def run(copies):
    for copy in copies:
        copy.start()
    for copy in copies:
        copy.wait()


def previous(block):
    count = lax.axis_size("sec")
    return lax.ppermute(block, "sec", [((i + 1) % count, i) for i in range(count)])


def swapped(block, distance):
    return lax.ppermute(block, "slab", [(i, i ^ distance) for i in range(lax.axis_size("slab"))])


def part_copies(blocks, unit, place, basis, array, sems):
    slabs = lax.axis_size("slab")
    rows = basis.shape[1] // slabs
    copies = []
    for at, (sector, start) in enumerate(blocks):
        for slab in range(slabs // 2):
            row = pl.multiple_of((2 * slab + place[0] % 2) * rows, rows)
            copies.append(
                pltpu.make_async_copy(
                    basis.at[sector, pl.ds(row, rows), pl.ds(first_column(start, place, unit), unit)],
                    array.at[at, pl.ds(slab * rows, rows)],
                    sems.at[len(copies)],
                )
            )
    return copies


def half_products(sectors, distances, place, basis, fermion, pieces, ready=lambda sector: None):
    flavours, _, _, width = fermion.shape
    for sector in sectors:
        ready(sector)
        right = jnp.concatenate([fermion[flavour, sector] for flavour in range(flavours)], axis=1)
        for slot, distance in enumerate(distances):
            column = pl.multiple_of((place[0] ^ distance) * width, width)
            block = lax.dot_general(
                basis[sector, :, pl.ds(column, width)],
                right,
                (((0,), (0,)), ((), ())),
                preferred_element_type=jnp.float32,
            ).astype(jnp.bfloat16)
            for flavour in range(flavours):
                pieces[slot][sector, flavour] = block[:, flavour * width : (flavour + 1) * width]


def part_kernel(blocks, unit, distances, place, basis, fermion, sent, *refs):
    *pieces, left, right, sems, half_sems = refs
    copies = part_copies(blocks, unit, place, basis, sent, sems)
    for copy in copies:
        copy.start()

    @pl.when(place[1] == 0)
    def _():
        held = [
            [
                pltpu.make_async_copy(basis.at[sector], left.at[sector], half_sems.at[sector, 0]),
                pltpu.make_async_copy(fermion.at[:, sector], right.at[:, sector], half_sems.at[sector, 1]),
            ]
            for sector in range(basis.shape[0])
        ]
        for pair in held:
            for copy in pair:
                copy.start()

        def ready(sector):
            for copy in held[sector]:
                copy.wait()

        half_products(range(basis.shape[0]), distances, place, left, right, pieces, ready)

    for copy in copies:
        copy.wait()


def basis_part(basis, fermion, blocks, unit, distances):
    flavours, sectors, depth, width = fermion.shape
    shapes = [pltpu.VMEM((len(blocks), depth // 2, unit), jnp.bfloat16)]
    shapes += [pltpu.VMEM((sectors, flavours, width, width), jnp.bfloat16)] * len(distances)
    return kernel_call(
        functools.partial(part_kernel, blocks, unit, distances),
        "part",
        basis.shape[:2],
        [in_hbm(basis), in_hbm(fermion)],
        [ANY, ANY],
        shapes,
        [WHOLE] * len(shapes),
        [
            pltpu.VMEM((sectors, depth, depth), jnp.bfloat16),
            pltpu.VMEM((flavours, sectors, depth, width), jnp.bfloat16),
            pltpu.SemaphoreType.DMA((len(blocks) * lax.axis_size("slab") // 2,)),
            pltpu.SemaphoreType.DMA((sectors, 2)),
        ],
    )


def far_kernel(distances, place, basis, fermion, *refs):
    pieces = refs[len(distances) :]

    @pl.when(place[1] != 0)
    def _():
        half_products(range(basis.shape[0]), distances, place, basis, fermion, pieces)


def far_blocks(basis, fermion, distances, earlier):
    return kernel_call(
        functools.partial(far_kernel, distances),
        "far",
        basis.shape[:2],
        [in_vmem(basis), in_vmem(fermion), *map(in_vmem, earlier)],
        [WHOLE] * (2 + len(earlier)),
        [pltpu.VMEM(piece.shape, piece.dtype) for piece in earlier],
        [WHOLE] * len(distances),
        aliases={2 + at: at for at in range(len(earlier))},
    )


def near_kernel(blocks, unit, distances, place, basis, fermion, _, *refs):
    *pieces, sent, sems = refs
    copies = part_copies(blocks, unit, place, basis, sent, sems)
    for copy in copies:
        copy.start()
    half_products(range(basis.shape[0]), distances, place, basis, fermion, pieces)
    for copy in copies:
        copy.wait()


def near_blocks(basis, fermion, blocks, unit, distances, after):
    flavours, sectors, depth, width = fermion.shape
    return kernel_call(
        functools.partial(near_kernel, blocks, unit, distances),
        "near",
        basis.shape[:2],
        [in_vmem(basis), in_vmem(fermion), in_vmem(after)],
        [WHOLE, WHOLE, WHOLE],
        [pltpu.VMEM((sectors, flavours, width, width), jnp.bfloat16)] * len(distances)
        + [pltpu.VMEM((len(blocks), depth // 2, unit), jnp.bfloat16)],
        [WHOLE] * (len(distances) + 1),
        [pltpu.SemaphoreType.DMA((len(blocks) * lax.axis_size("slab") // 2,))],
    )


def cut_kernel(cuts, given, *refs):
    for cut, piece in zip(cuts, refs[-len(cuts) :]):
        piece[...] = given[cut]


def cut_out(array, cuts, after=()):
    shapes = [jax.eval_shape(lambda x, cut=cut: x[cut], array).shape for cut in cuts]
    return kernel_call(
        functools.partial(cut_kernel, cuts),
        "cut",
        None,
        [in_vmem(array), *map(in_vmem, after)],
        [WHOLE] * (1 + len(after)),
        [pltpu.VMEM(shape, array.dtype) for shape in shapes],
        [WHOLE] * len(cuts),
    )


def own_copies(units, unit, place, basis, right, sems, first):
    sectors, depth, _ = basis.shape
    slabs = lax.axis_size("slab")
    rows = depth // slabs
    copies, at = [], 0
    for start, count in units:
        for slab in range(slabs):
            to = ((slab % 2) * (slabs // 2) + slab // 2) * rows
            copies.append(
                pltpu.make_async_copy(
                    basis.at[:, pl.ds(slab * rows, rows), pl.ds(first_column(start, place, unit), count * unit)],
                    right.at[pl.ds(0, sectors), pl.ds(to, rows), pl.ds(at, count * unit)],
                    sems.at[first + len(copies)],
                )
            )
        at += count * unit
    return copies


def next_copies(nexts, place, pairs, right, sems, first):
    sectors, depth = right.shape[0] // 2, right.shape[1]
    copies = []
    for pair, holds in zip(pairs, nexts):
        for index, many, sector, column in holds:
            for side in range(2):
                to = pl.multiple_of(((place[0] + side) % 2) * (depth // 2), depth // 2)
                copies.append(
                    pltpu.make_async_copy(
                        pair[side].at[pl.ds(index, many)],
                        right.at[
                            pl.ds(sectors + sector, many), pl.ds(to, depth // 2), pl.ds(column, pair[side].shape[2])
                        ],
                        sems.at[first + len(copies)],
                    )
                )
    return copies


def half_copy(half, distance, place, left, sem):
    slabs = lax.axis_size("slab")
    width = half.shape[3]
    slab = place[0] ^ distance
    column = pl.multiple_of(((slab % 2) * (slabs // 2) + slab // 2) * width, width)
    return pltpu.make_async_copy(half, left.at[:, :, :, pl.ds(column, width)], sem)


def gather_kernel(early_units, late_units, nexts, unit, distances, cut, place, basis, *refs):
    halves, refs = refs[: len(distances)], refs[len(distances) :]
    pairs, refs = [refs[2 * i : 2 * i + 2] for i in range(len(nexts))], refs[2 * len(nexts) :]
    left, early_right, late_right, sent, sems = refs
    copies = own_copies(early_units, unit, place, basis, early_right, sems, 0)
    copies += next_copies(nexts, place, pairs, early_right, sems, len(copies))
    copies += own_copies(late_units, unit, place, basis, late_right, sems, len(copies))
    for half, distance in zip(halves, distances):
        copies.append(half_copy(half, distance, place, left, sems.at[len(copies)]))
    copies.append(pltpu.make_async_copy(pairs[-1][0].at[cut], sent, sems.at[len(copies)]))
    run(copies)


def gather(basis, early_units, late_units, nexts, unit, pairs, halves, distances, cut):
    sectors, depth, _ = basis.shape
    flavours, width = halves[0].shape[1:3]
    given = [in_vmem(array) for array in (basis, *halves, *(array for pair in pairs for array in pair))]
    early_columns, late_columns = (sum(count for _, count in units) * unit for units in (early_units, late_units))
    copies = (len(early_units) + len(late_units)) * (depth // width) + 2 * sum(len(holds) for holds in nexts)
    last = pairs[-1][0]
    return kernel_call(
        functools.partial(gather_kernel, early_units, late_units, nexts, unit, distances, cut),
        "gather",
        basis.shape[:2],
        given,
        [WHOLE] * len(given),
        [
            pltpu.VMEM((sectors, flavours, width, depth), jnp.bfloat16),
            pltpu.VMEM((2 * sectors, depth, early_columns), jnp.bfloat16),
            pltpu.VMEM((2 * sectors, depth, late_columns), jnp.bfloat16),
            pltpu.VMEM((cut.size, *last.shape[1:]), jnp.bfloat16),
        ],
        [WHOLE] * 4,
        [pltpu.SemaphoreType.DMA((copies + len(halves) + 1,))],
    )


def product(place, partner, sector, flavour, left, right):
    index = (partner[...][sector, flavour] - place[1] + place[2]) % place[2]
    return jnp.dot(left[sector, flavour], right[index], preferred_element_type=jnp.float32).astype(jnp.bfloat16)


def early_kernel(distance, place, partner, half, right, _, left, stage, sem):
    run([half_copy(half, distance, place, left, sem)])
    sectors, flavours = left.shape[:2]
    for sector in range(sectors):
        for flavour in range(flavours):
            stage[flavour, sector] = product(place, partner, sector, flavour, left, right)


def early_products(partner, half, distance, left, right):
    sectors, flavours, width, _ = left.shape
    return kernel_call(
        functools.partial(early_kernel, distance),
        "early",
        (left.shape[0], left.shape[3]),
        [partner, in_vmem(half), in_vmem(right), in_vmem(left)],
        [WHOLE] + [WHOLE] * 3,
        [
            pltpu.VMEM(left.shape, left.dtype),
            pltpu.VMEM((flavours, sectors, width, right.shape[2]), jnp.bfloat16),
        ],
        [WHOLE] * 2,
        [pltpu.SemaphoreType.DMA],
        {3: 0},
    )


def late_kernel(early_units, units, nexts, unit, place, partner, left, early, *refs):
    pairs, refs = [refs[2 * i : 2 * i + 2] for i in range(len(nexts))], refs[2 * len(nexts) :]
    _, out, right, stage, sems, early_sems, out_sems = refs
    sectors, flavours = left.shape[:2]
    next_here = next_copies(nexts, place, pairs, right, sems, 0)
    for copy in next_here:
        copy.start()
    out_copies, at = [], 0
    for start, count in early_units:
        out_copies.append(
            pltpu.make_async_copy(
                early.at[:, :, :, pl.ds(at, count * unit)],
                out.at[:, :, :, pl.ds(first_column(start, place, unit), count * unit)],
                early_sems.at[len(out_copies)],
            )
        )
        out_copies[-1].start()
        at += count * unit
    for copy in next_here:
        copy.wait()
    for sector in range(sectors):
        for flavour in range(flavours):
            stage[flavour, sector] = product(place, partner, sector, flavour, left, right)
            at = 0
            for number, (start, count) in enumerate(units):
                copy = pltpu.make_async_copy(
                    stage.at[flavour, sector, :, pl.ds(at, count * unit)],
                    out.at[flavour, sector, :, pl.ds(first_column(start, place, unit), count * unit)],
                    out_sems.at[sector * flavours + flavour, number],
                )
                copy.start()
                out_copies.append(copy)
                at += count * unit
    for copy in out_copies:
        copy.wait()


def late_products(partner, early_units, units, nexts, unit, pairs, left, early, right):
    sectors, flavours, width, depth = left.shape
    given = [in_vmem(array) for array in (left, early, *(array for pair in pairs for array in pair), right)]
    return kernel_call(
        functools.partial(late_kernel, early_units, units, nexts, unit),
        "late",
        (sectors, depth),
        [partner, *given],
        [WHOLE] + [WHOLE] * len(given),
        [
            pltpu.HBM((flavours, sectors, width, depth), jnp.bfloat16),
            pltpu.VMEM(right.shape, right.dtype),
        ],
        [ANY, WHOLE],
        [
            pltpu.VMEM((flavours, sectors, width, right.shape[2]), jnp.bfloat16),
            pltpu.SemaphoreType.DMA((2 * sum(len(holds) for holds in nexts),)),
            pltpu.SemaphoreType.DMA((len(early_units),)),
            pltpu.SemaphoreType.DMA((sectors * flavours, len(units))),
        ],
        {len(given): 1},
    )[0]


def local(basis, fermion, partner):
    sectors, depth, _ = basis.shape
    unit = depth // 8
    partner = partner.T
    distances = (3, 2, 1, 0)
    alone = sectors // 2
    count = 3
    early_units, late_units = ((0, count), (OWN, 1)), ((count, 6 - count), (OTHER, 1))
    first_blocks = [(sector, start) for start in (*range(count), OWN) for sector in range(sectors)]
    last_blocks = [(sector, start) for start in range(count, 6) for sector in range(sectors)]
    last_blocks += [(sector, OTHER) for sector in range(alone)]
    first_part, *far = basis_part(basis, fermion, first_blocks, unit, distances[:2])
    first = previous(first_part)
    far3, far2 = far_blocks(basis, fermion, distances[:2], far)
    got2, got3 = swapped(far2, 2), swapped(far3, 3)
    mine, near, last_part = near_blocks(basis, fermion, last_blocks, unit, distances[2:], far2)
    beside, last = swapped(mine, 1), previous(last_part)
    groups = ((0, 2), (2, 4))
    pieces = cut_out(first, [slice(begin * sectors, end * sectors) for begin, end in groups], (beside, got2))
    pairs = [(piece, swapped(piece, 1)) for piece in pieces]
    nexts = [
        [((at - begin) * sectors, sectors, 0, at * unit) for at in range(begin, end)] for begin, end in groups
    ]
    begin, end = groups[-1]
    cut = pl.ds((end - 1 - begin) * sectors + alone, sectors - alone)
    left, early_right, late_right, sent = gather(
        basis, early_units, late_units, nexts, unit, pairs, [got2, beside, near], distances[1:], cut
    )
    other = swapped(sent, 2)
    left, early = early_products(partner, got3, distances[0], left, early_right)
    nexts = [[(at * sectors, sectors, 0, at * unit) for at in range(6 - count)]]
    if alone:
        nexts[0].append(((6 - count) * sectors, alone, 0, (6 - count) * unit))
    nexts.append([(0, sectors - alone, alone, (6 - count) * unit)])
    last, other, early = lax.optimization_barrier((last, other, early))
    pairs = [(last, swapped(last, 1)), (other, swapped(other, 1))]
    return late_products(partner, early_units, late_units, nexts, unit, pairs, left, early, late_right)


def solution(mesh):
    placed = (P("sec", None, None), P(None, "sec", None, "slab"), P(None, "sec"))
    return jax.shard_map(
        local, mesh=mesh, in_specs=placed, out_specs=P(None, "sec", "slab", None), check_vma=False
    )
```

```python
import functools

import jax
import jax.numpy as jnp
from jax import lax
from jax.experimental import pallas as pl
from jax.experimental.pallas import tpu as pltpu
from jax.sharding import PartitionSpec as P

ANY = pl.BlockSpec(memory_space=pl.ANY)
WHOLE = pl.BlockSpec(memory_space=pltpu.VMEM)
OWN, OTHER = -1, -2
KERNEL_BYTES = 16 * 1024 * 1024
BRIEF = pl.CostEstimate(flops=0, bytes_accessed=0, transcendentals=0)


def in_hbm(array):
    return pltpu.with_memory_space_constraint(array, pltpu.HBM)


def in_vmem(array):
    return pltpu.with_memory_space_constraint(array, pltpu.VMEM)


def located(sectors, depth):
    first = lax.axis_index("sec") * sectors
    return lax.axis_index("slab"), first, lax.axis_size("sec") * sectors, depth - depth // 8 * 2


def kernel_call(body, name, shape, given, specs, shapes, out_specs, scratch=(), aliases={}, cost=BRIEF):
    def kernel(*refs):
        body(*(() if shape is None else (located(*shape),)), *refs)

    return pl.pallas_call(
        kernel,
        out_shape=shapes,
        in_specs=specs,
        out_specs=out_specs,
        scratch_shapes=list(scratch),
        input_output_aliases=aliases,
        compiler_params=pltpu.CompilerParams(vmem_limit_bytes=KERNEL_BYTES),
        cost_estimate=cost,
        name=name,
    )(*given)


def first_column(unit, place, width):
    if unit == OWN:
        return pl.multiple_of(place[3] + (place[0] // 2) * width, width)
    if unit == OTHER:
        return pl.multiple_of(place[3] + (1 - place[0] // 2) * width, width)
    return unit * width


def run(copies):
    for copy in copies:
        copy.start()
    for copy in copies:
        copy.wait()


def previous(block):
    count = lax.axis_size("sec")
    return lax.ppermute(block, "sec", [((i + 1) % count, i) for i in range(count)])


def swapped(block, distance):
    return lax.ppermute(block, "slab", [(i, i ^ distance) for i in range(lax.axis_size("slab"))])


def part_copies(blocks, unit, place, basis, array, sems):
    rows = basis.shape[1] // lax.axis_size("slab")
    copies = []
    for at, (sector, start, slab) in enumerate(blocks):
        row = pl.multiple_of((2 * slab + place[0] % 2) * rows, rows)
        copies.append(
            pltpu.make_async_copy(
                basis.at[sector, pl.ds(row, rows), pl.ds(first_column(start, place, unit), unit)],
                array.at[at],
                sems.at[len(copies)],
            )
        )
    return copies


def half_products(sectors, distances, place, basis, fermion, pieces, ready=lambda sector: None):
    flavours, _, _, width = fermion.shape
    for sector in sectors:
        ready(sector)
        right = jnp.concatenate([fermion[flavour, sector] for flavour in range(flavours)], axis=1)
        for slot, distance in enumerate(distances):
            column = pl.multiple_of((place[0] ^ distance) * width, width)
            block = lax.dot_general(
                basis[sector, :, pl.ds(column, width)],
                right,
                (((0,), (0,)), ((), ())),
                preferred_element_type=jnp.float32,
            ).astype(jnp.bfloat16)
            for flavour in range(flavours):
                pieces[slot][sector, flavour] = block[:, flavour * width : (flavour + 1) * width]


def part_kernel(blocks, unit, distances, place, basis, fermion, sent, *refs):
    *pieces, left, right, sems, half_sems = refs
    copies = part_copies(blocks, unit, place, basis, sent, sems)
    for copy in copies:
        copy.start()

    @pl.when(place[1] == 0)
    def _():
        held = [
            [
                pltpu.make_async_copy(basis.at[sector], left.at[sector], half_sems.at[sector, 0]),
                pltpu.make_async_copy(fermion.at[:, sector], right.at[:, sector], half_sems.at[sector, 1]),
            ]
            for sector in range(basis.shape[0])
        ]
        for pair in held:
            for copy in pair:
                copy.start()

        def ready(sector):
            for copy in held[sector]:
                copy.wait()

        half_products(range(basis.shape[0]), distances, place, left, right, pieces, ready)

    for copy in copies:
        copy.wait()


def basis_part(basis, fermion, blocks, unit, distances):
    flavours, sectors, depth, width = fermion.shape
    shapes = [pltpu.VMEM((len(blocks), width, unit), jnp.bfloat16)]
    shapes += [pltpu.VMEM((sectors, flavours, width, width), jnp.bfloat16)] * len(distances)
    return kernel_call(
        functools.partial(part_kernel, blocks, unit, distances),
        "part",
        basis.shape[:2],
        [in_hbm(basis), in_hbm(fermion)],
        [ANY, ANY],
        shapes,
        [WHOLE] * len(shapes),
        [
            pltpu.VMEM((sectors, depth, depth), jnp.bfloat16),
            pltpu.VMEM((flavours, sectors, depth, width), jnp.bfloat16),
            pltpu.SemaphoreType.DMA((len(blocks),)),
            pltpu.SemaphoreType.DMA((sectors, 2)),
        ],
    )


def far_kernel(distances, place, basis, fermion, *refs):
    pieces = refs[len(distances) :]

    @pl.when(place[1] != 0)
    def _():
        half_products(range(basis.shape[0]), distances, place, basis, fermion, pieces)


def far_blocks(basis, fermion, distances, earlier):
    return kernel_call(
        functools.partial(far_kernel, distances),
        "far",
        basis.shape[:2],
        [in_vmem(basis), in_vmem(fermion), *map(in_vmem, earlier)],
        [WHOLE] * (2 + len(earlier)),
        [pltpu.VMEM(piece.shape, piece.dtype) for piece in earlier],
        [WHOLE] * len(distances),
        aliases={2 + at: at for at in range(len(earlier))},
    )


def near_kernel(blocks, unit, distances, place, basis, fermion, _, *refs):
    *pieces, sent, sems = refs
    copies = part_copies(blocks, unit, place, basis, sent, sems)
    for copy in copies:
        copy.start()
    half_products(range(basis.shape[0]), distances, place, basis, fermion, pieces)
    for copy in copies:
        copy.wait()


def near_blocks(basis, fermion, blocks, unit, distances, after):
    flavours, sectors, depth, width = fermion.shape
    return kernel_call(
        functools.partial(near_kernel, blocks, unit, distances),
        "near",
        basis.shape[:2],
        [in_vmem(basis), in_vmem(fermion), in_vmem(after)],
        [WHOLE, WHOLE, WHOLE],
        [pltpu.VMEM((sectors, flavours, width, width), jnp.bfloat16)] * len(distances)
        + [pltpu.VMEM((len(blocks), width, unit), jnp.bfloat16)],
        [WHOLE] * (len(distances) + 1),
        [pltpu.SemaphoreType.DMA((len(blocks),))],
    )


def cut_kernel(cuts, given, *refs):
    for cut, piece in zip(cuts, refs[-len(cuts) :]):
        piece[...] = given[cut]


def cut_out(array, cuts, after=()):
    shapes = [jax.eval_shape(lambda x, cut=cut: x[cut], array).shape for cut in cuts]
    return kernel_call(
        functools.partial(cut_kernel, cuts),
        "cut",
        None,
        [in_vmem(array), *map(in_vmem, after)],
        [WHOLE] * (1 + len(after)),
        [pltpu.VMEM(shape, array.dtype) for shape in shapes],
        [WHOLE] * len(cuts),
    )


def own_copies(units, unit, place, basis, right, sems, first):
    sectors, depth, _ = basis.shape
    slabs = lax.axis_size("slab")
    rows = depth // slabs
    copies, at = [], 0
    for start, count in units:
        for slab in range(slabs):
            to = ((slab % 2) * (slabs // 2) + slab // 2) * rows
            copies.append(
                pltpu.make_async_copy(
                    basis.at[:, pl.ds(slab * rows, rows), pl.ds(first_column(start, place, unit), count * unit)],
                    right.at[pl.ds(0, sectors), pl.ds(to, rows), pl.ds(at, count * unit)],
                    sems.at[first + len(copies)],
                )
            )
        at += count * unit
    return copies


def next_copies(nexts, place, arrays, side, right, sems, first):
    sectors, depth = right.shape[0] // 2, right.shape[1]
    copies = []
    for array, blocks in zip(arrays, nexts):
        _, rows, columns = array.shape
        for index, (sector, slab, column) in enumerate(blocks):
            to = pl.multiple_of(((place[0] + side) % 2) * (depth // 2) + slab * rows, rows)
            copies.append(
                pltpu.make_async_copy(
                    array.at[index],
                    right.at[sectors + sector, pl.ds(to, rows), pl.ds(column, columns)],
                    sems.at[first + len(copies)],
                )
            )
    return copies


def half_copy(half, distance, place, left, sem):
    slabs = lax.axis_size("slab")
    width = half.shape[3]
    slab = place[0] ^ distance
    column = pl.multiple_of(((slab % 2) * (slabs // 2) + slab // 2) * width, width)
    return pltpu.make_async_copy(half, left.at[:, :, :, pl.ds(column, width)], sem)


def gather_kernel(groups, nexts, unit, distances, cuts, place, basis, *refs):
    halves, refs = refs[: len(distances)], refs[len(distances) :]
    pairs, refs = [refs[2 * i : 2 * i + 2] for i in range(len(nexts))], refs[2 * len(nexts) :]
    left, *rights, sent, sems = refs
    copies = next_copies(nexts, place, [pair[0] for pair in pairs], 0, rights[0], sems, 0)
    copies += next_copies(nexts, place, [pair[1] for pair in pairs], 1, rights[0], sems, len(copies))
    for units, right in zip(groups, rights):
        copies += own_copies(units, unit, place, basis, right, sems, len(copies))
    for half, distance in zip(halves, distances):
        copies.append(half_copy(half, distance, place, left, sems.at[len(copies)]))
    for at, cut in enumerate(cuts):
        copies.append(pltpu.make_async_copy(pairs[-1][0].at[cut], sent.at[at], sems.at[len(copies)]))
    run(copies)


def gather(basis, groups, nexts, unit, pairs, halves, distances, cuts):
    sectors, depth, _ = basis.shape
    flavours, width = halves[0].shape[1:3]
    given = [in_vmem(array) for array in (basis, *halves, *(array for pair in pairs for array in pair))]
    copies = sum(map(len, groups)) * (depth // width) + 2 * sum(len(holds) for holds in nexts)
    last = pairs[-1][0]
    shapes = [pltpu.VMEM((sectors, flavours, width, depth), jnp.bfloat16)]
    for units in groups:
        shapes.append(pltpu.VMEM((2 * sectors, depth, sum(count for _, count in units) * unit), jnp.bfloat16))
    shapes.append(pltpu.VMEM((len(cuts), *last.shape[1:]), jnp.bfloat16))
    return kernel_call(
        functools.partial(gather_kernel, groups, nexts, unit, distances, cuts),
        "gather",
        basis.shape[:2],
        given,
        [WHOLE] * len(given),
        shapes,
        [WHOLE] * len(shapes),
        [pltpu.SemaphoreType.DMA((copies + len(halves) + len(cuts),))],
    )


def product(place, partner, sector, flavour, left, right):
    index = (partner[...][sector, flavour] - place[1] + place[2]) % place[2]
    return jnp.dot(left[sector, flavour], right[index], preferred_element_type=jnp.float32).astype(jnp.bfloat16)


def early_kernel(distance, place, partner, half, right, _, left, stage, sem):
    run([half_copy(half, distance, place, left, sem)])
    sectors, flavours = left.shape[:2]
    for sector in range(sectors):
        for flavour in range(flavours):
            stage[flavour, sector] = product(place, partner, sector, flavour, left, right)


def early_products(partner, half, distance, left, right):
    sectors, flavours, width, _ = left.shape
    return kernel_call(
        functools.partial(early_kernel, distance),
        "early",
        (left.shape[0], left.shape[3]),
        [partner, in_vmem(half), in_vmem(right), in_vmem(left)],
        [WHOLE] + [WHOLE] * 3,
        [
            pltpu.VMEM(left.shape, left.dtype),
            pltpu.VMEM((flavours, sectors, width, right.shape[2]), jnp.bfloat16),
        ],
        [WHOLE] * 2,
        [pltpu.SemaphoreType.DMA],
        {3: 0},
    )


def partial(place, partner, sector, flavour, side, left, right):
    index = (partner[...][sector, flavour] - place[1] + place[2]) % place[2]
    depth = right.shape[1]
    half = pl.ds(pl.multiple_of(((place[0] + side) % 2) * (depth // 2), depth // 2), depth // 2)
    return jnp.dot(left[sector, flavour, :, half], right[index, half, :], preferred_element_type=jnp.float32)


def own_rows_kernel(groups, place, partner, left, *refs):
    arrays = []
    for nexts in groups:
        arrays.append(refs[: len(nexts)])
        refs = refs[len(nexts) :]
    refs = refs[len(groups) :]
    totals, rights, sems = refs[: len(groups)], refs[len(groups) : 2 * len(groups)], refs[2 * len(groups) :]
    copies = [
        next_copies(nexts, place, here, 0, right, sem, 0)
        for nexts, here, right, sem in zip(groups, arrays, rights, sems)
    ]
    for group in copies:
        for copy in group:
            copy.start()
    sectors, flavours = left.shape[:2]
    for group, total, right in zip(copies, totals, rights):
        for copy in group:
            copy.wait()
        for sector in range(sectors):
            for flavour in range(flavours):
                total[flavour, sector] = partial(place, partner, sector, flavour, 0, left, right)


def own_rows(partner, groups, arrays, left, rights):
    sectors, flavours, width, depth = left.shape
    given = [in_vmem(array) for array in (left, *(array for group in arrays for array in group), *rights)]
    first = 1 + len(given) - len(rights)
    return kernel_call(
        functools.partial(own_rows_kernel, groups),
        "own_rows",
        (sectors, depth),
        [partner, *given],
        [WHOLE] * (1 + len(given)),
        [pltpu.VMEM((flavours, sectors, width, right.shape[2]), jnp.float32) for right in rights]
        + [pltpu.VMEM(right.shape, right.dtype) for right in rights],
        [WHOLE] * (2 * len(rights)),
        [pltpu.SemaphoreType.DMA((sum(map(len, nexts)),)) for nexts in groups],
        {first + at: len(rights) + at for at in range(len(rights))},
    )


def late_kernel(earlier_units, units, nexts, unit, place, partner, left, total, *refs):
    earlier, refs = refs[: len(earlier_units)], refs[len(earlier_units) :]
    arrays, (_, out, right, stage, sems, early_sems, out_sems) = refs[: len(nexts)], refs[len(nexts) :]
    sectors, flavours = left.shape[:2]
    next_here = next_copies(nexts, place, arrays, 1, right, sems, 0)
    for copy in next_here:
        copy.start()
    out_copies = []
    for result, spans in zip(earlier, earlier_units):
        at = 0
        for start, count in spans:
            out_copies.append(
                pltpu.make_async_copy(
                    result.at[:, :, :, pl.ds(at, count * unit)],
                    out.at[:, :, :, pl.ds(first_column(start, place, unit), count * unit)],
                    early_sems.at[len(out_copies)],
                )
            )
            out_copies[-1].start()
            at += count * unit
    for copy in next_here:
        copy.wait()
    for sector in range(sectors):
        for flavour in range(flavours):
            rest = partial(place, partner, sector, flavour, 1, left, right)
            stage[flavour, sector] = (total[flavour, sector] + rest).astype(jnp.bfloat16)
            at = 0
            for number, (start, count) in enumerate(units):
                copy = pltpu.make_async_copy(
                    stage.at[flavour, sector, :, pl.ds(at, count * unit)],
                    out.at[flavour, sector, :, pl.ds(first_column(start, place, unit), count * unit)],
                    out_sems.at[sector * flavours + flavour, number],
                )
                copy.start()
                out_copies.append(copy)
                at += count * unit
    for copy in out_copies:
        copy.wait()


def late_products(partner, groups, nexts, unit, arrays, left, total, earlier, right):
    sectors, flavours, width, depth = left.shape
    given = [in_vmem(array) for array in (left, total, *earlier, *arrays, right)]
    return kernel_call(
        functools.partial(late_kernel, groups[:-1], groups[-1], nexts, unit),
        "late",
        (sectors, depth),
        [partner, *given],
        [WHOLE] * (1 + len(given)),
        [
            pltpu.HBM((flavours, sectors, width, depth), jnp.bfloat16),
            pltpu.VMEM(right.shape, right.dtype),
        ],
        [ANY, WHOLE],
        [
            pltpu.VMEM((flavours, sectors, width, right.shape[2]), jnp.bfloat16),
            pltpu.SemaphoreType.DMA((sum(map(len, nexts)),)),
            pltpu.SemaphoreType.DMA((sum(map(len, groups[:-1])),)),
            pltpu.SemaphoreType.DMA((sectors * flavours, len(groups[-1]))),
        ],
        {len(given): 1},
    )[0]


def local(basis, fermion, partner):
    sectors, depth, _ = basis.shape
    unit = depth // 8
    partner = partner.T
    distances = (3, 2, 1, 0)
    slabs = range(lax.axis_size("slab") // 2)
    held = [(sector, slab) for sector in range(sectors) for slab in slabs]
    alone = len(held) // 4
    count = 3
    units = ((0, count), (OWN, 1)), ((count, 6 - count), (OTHER, 1))
    first_blocks = [(sector, start, slab) for start in (*range(count), OWN) for sector, slab in held]
    last_blocks = [(sector, start, slab) for start in range(count, 6) for sector, slab in held]
    last_blocks += [(sector, OTHER, slab) for sector, slab in held[:alone]]
    first_part, *far = basis_part(basis, fermion, first_blocks, unit, distances[:2])
    first = previous(first_part)
    far3, far2 = far_blocks(basis, fermion, distances[:2], far)
    got2, got3 = swapped(far2, 2), swapped(far3, 3)
    mine, near, last_part = near_blocks(basis, fermion, last_blocks, unit, distances[2:], far2)
    beside, last = swapped(mine, 1), previous(last_part)

    def columns(begin, end):
        return [(sector, slab, at * unit) for at in range(begin, end) for sector, slab in held]

    groups = ((0, 2), (2, 4))
    pieces = cut_out(first, [slice(begin * len(held), end * len(held)) for begin, end in groups], (beside, got2))
    pairs = [(piece, swapped(piece, 1)) for piece in pieces]
    nexts = [columns(*group) for group in groups]
    cuts = range(len(nexts[-1]) - len(held) + alone, len(nexts[-1]))
    left, early_right, late_right, sent = gather(
        basis, units, nexts, unit, pairs, [got2, beside, near], distances[1:], cuts
    )
    other = swapped(sent, 2)
    left, early = early_products(partner, got3, distances[0], left, early_right)
    last, other, early = lax.optimization_barrier((last, other, early))
    last_other, other_other = swapped(last, 1), swapped(other, 1)
    full = columns(0, 6 - count + 1)
    split = len(full) - len(held) + alone
    nexts = [full[:split], full[split:]]
    total, late_right = own_rows(partner, [nexts], [[last, other]], left, [late_right])
    return late_products(
        partner, units, nexts, unit, [last_other, other_other], left, total, [early], late_right
    )


def solution(mesh):
    placed = (P("sec", None, None), P(None, "sec", None, "slab"), P(None, "sec"))
    return jax.shard_map(
        local, mesh=mesh, in_specs=placed, out_specs=P(None, "sec", "slab", None), check_vma=False
    )
```

```python
import functools

import jax
import jax.numpy as jnp
from jax import lax
from jax.experimental import pallas as pl
from jax.experimental.pallas import tpu as pltpu
from jax.sharding import PartitionSpec as P

ANY = pl.BlockSpec(memory_space=pl.ANY)
WHOLE = pl.BlockSpec(memory_space=pltpu.VMEM)
OWN, OTHER = -1, -2
KERNEL_BYTES = 16 * 1024 * 1024
BRIEF = pl.CostEstimate(flops=0, bytes_accessed=0, transcendentals=0)


def in_hbm(array):
    return pltpu.with_memory_space_constraint(array, pltpu.HBM)


def in_vmem(array):
    return pltpu.with_memory_space_constraint(array, pltpu.VMEM)


def located(sectors, depth):
    first = lax.axis_index("sec") * sectors
    return lax.axis_index("slab"), first, lax.axis_size("sec") * sectors, depth - depth // 8 * 2


def kernel_call(body, name, shape, given, specs, shapes, out_specs, scratch=(), aliases={}, cost=BRIEF):
    def kernel(*refs):
        body(*(() if shape is None else (located(*shape),)), *refs)

    return pl.pallas_call(
        kernel,
        out_shape=shapes,
        in_specs=specs,
        out_specs=out_specs,
        scratch_shapes=list(scratch),
        input_output_aliases=aliases,
        compiler_params=pltpu.CompilerParams(vmem_limit_bytes=KERNEL_BYTES),
        cost_estimate=cost,
        name=name,
    )(*given)


def first_column(unit, place, width):
    if unit == OWN:
        return pl.multiple_of(place[3] + (place[0] // 2) * width, width)
    if unit == OTHER:
        return pl.multiple_of(place[3] + (1 - place[0] // 2) * width, width)
    return unit * width


def run(copies):
    for copy in copies:
        copy.start()
    for copy in copies:
        copy.wait()


def previous(block):
    count = lax.axis_size("sec")
    return lax.ppermute(block, "sec", [((i + 1) % count, i) for i in range(count)])


def swapped(block, distance):
    return lax.ppermute(block, "slab", [(i, i ^ distance) for i in range(lax.axis_size("slab"))])


def part_copies(blocks, unit, place, basis, array, sems):
    rows = basis.shape[1] // lax.axis_size("slab")
    copies = []
    for at, (sector, spans, slab) in enumerate(blocks):
        row = pl.multiple_of((2 * slab + place[0] % 2) * rows, rows)
        column = 0
        for start, count in spans:
            copies.append(
                pltpu.make_async_copy(
                    basis.at[sector, pl.ds(row, rows), pl.ds(first_column(start, place, unit), count * unit)],
                    array.at[at, :, pl.ds(column, count * unit)],
                    sems.at[len(copies)],
                )
            )
            column += count * unit
    return copies


def part_shape(blocks, rows, unit):
    return pltpu.VMEM((len(blocks), rows, sum(count for _, count in blocks[0][1]) * unit), jnp.bfloat16)


def part_sems(blocks):
    return pltpu.SemaphoreType.DMA((sum(len(spans) for _, spans, _ in blocks),))


def half_products(sectors, distances, place, basis, fermion, pieces, ready=lambda sector: None):
    flavours, _, _, width = fermion.shape
    for sector in sectors:
        ready(sector)
        right = jnp.concatenate([fermion[flavour, sector] for flavour in range(flavours)], axis=1)
        for slot, distance in enumerate(distances):
            column = pl.multiple_of((place[0] ^ distance) * width, width)
            block = lax.dot_general(
                basis[sector, :, pl.ds(column, width)],
                right,
                (((0,), (0,)), ((), ())),
                preferred_element_type=jnp.float32,
            ).astype(jnp.bfloat16)
            for flavour in range(flavours):
                pieces[slot][sector, flavour] = block[:, flavour * width : (flavour + 1) * width]


def part_kernel(blocks, unit, distances, place, basis, fermion, sent, *refs):
    *pieces, left, right, sems, half_sems = refs
    copies = part_copies(blocks, unit, place, basis, sent, sems)
    for copy in copies:
        copy.start()

    @pl.when(place[1] == 0)
    def _():
        held = [
            [
                pltpu.make_async_copy(basis.at[sector], left.at[sector], half_sems.at[sector, 0]),
                pltpu.make_async_copy(fermion.at[:, sector], right.at[:, sector], half_sems.at[sector, 1]),
            ]
            for sector in range(basis.shape[0])
        ]
        for pair in held:
            for copy in pair:
                copy.start()

        def ready(sector):
            for copy in held[sector]:
                copy.wait()

        half_products(range(basis.shape[0]), distances, place, left, right, pieces, ready)

    for copy in copies:
        copy.wait()


def basis_part(basis, fermion, blocks, unit, distances):
    flavours, sectors, depth, width = fermion.shape
    shapes = [part_shape(blocks, width, unit)]
    shapes += [pltpu.VMEM((sectors, flavours, width, width), jnp.bfloat16)] * len(distances)
    return kernel_call(
        functools.partial(part_kernel, blocks, unit, distances),
        "part",
        basis.shape[:2],
        [in_hbm(basis), in_hbm(fermion)],
        [ANY, ANY],
        shapes,
        [WHOLE] * len(shapes),
        [
            pltpu.VMEM((sectors, depth, depth), jnp.bfloat16),
            pltpu.VMEM((flavours, sectors, depth, width), jnp.bfloat16),
            part_sems(blocks),
            pltpu.SemaphoreType.DMA((sectors, 2)),
        ],
    )


def far_kernel(distances, place, basis, fermion, *refs):
    pieces = refs[len(distances) :]

    @pl.when(place[1] != 0)
    def _():
        half_products(range(basis.shape[0]), distances, place, basis, fermion, pieces)


def far_blocks(basis, fermion, distances, earlier):
    return kernel_call(
        functools.partial(far_kernel, distances),
        "far",
        basis.shape[:2],
        [in_vmem(basis), in_vmem(fermion), *map(in_vmem, earlier)],
        [WHOLE] * (2 + len(earlier)),
        [pltpu.VMEM(piece.shape, piece.dtype) for piece in earlier],
        [WHOLE] * len(distances),
        aliases={2 + at: at for at in range(len(earlier))},
    )


def near_kernel(blocks, unit, distances, place, basis, fermion, _, *refs):
    *pieces, sent, sems = refs
    copies = part_copies(blocks, unit, place, basis, sent, sems)
    for copy in copies:
        copy.start()
    half_products(range(basis.shape[0]), distances, place, basis, fermion, pieces)
    for copy in copies:
        copy.wait()


def near_blocks(basis, fermion, blocks, unit, distances, after):
    flavours, sectors, depth, width = fermion.shape
    return kernel_call(
        functools.partial(near_kernel, blocks, unit, distances),
        "near",
        basis.shape[:2],
        [in_vmem(basis), in_vmem(fermion), in_vmem(after)],
        [WHOLE, WHOLE, WHOLE],
        [pltpu.VMEM((sectors, flavours, width, width), jnp.bfloat16)] * len(distances)
        + [part_shape(blocks, width, unit)],
        [WHOLE] * (len(distances) + 1),
        [part_sems(blocks)],
    )


def cut_kernel(cuts, given, *refs):
    for cut, piece in zip(cuts, refs[-len(cuts) :]):
        piece[...] = given[cut]


def cut_out(array, cuts, after=()):
    shapes = [jax.eval_shape(lambda x, cut=cut: x[cut], array).shape for cut in cuts]
    return kernel_call(
        functools.partial(cut_kernel, cuts),
        "cut",
        None,
        [in_vmem(array), *map(in_vmem, after)],
        [WHOLE] * (1 + len(after)),
        [pltpu.VMEM(shape, array.dtype) for shape in shapes],
        [WHOLE] * len(cuts),
    )


def own_copies(units, unit, place, basis, right, sems, first):
    sectors, depth, _ = basis.shape
    slabs = lax.axis_size("slab")
    rows = depth // slabs
    copies, at = [], 0
    for start, count in units:
        for slab in range(slabs):
            copies.append(
                pltpu.make_async_copy(
                    basis.at[:, pl.ds(slab * rows, rows), pl.ds(first_column(start, place, unit), count * unit)],
                    right.at[pl.ds(0, sectors), slab % 2, slab // 2, :, pl.ds(at, count * unit)],
                    sems.at[first + len(copies)],
                )
            )
        at += count * unit
    return copies


def next_copies(nexts, place, arrays, side, right, sems, first):
    sectors = right.shape[0] // 2
    copies = []
    for array, runs in zip(arrays, nexts):
        index = 0
        for sector, slab, count, column in runs:
            copies.append(
                pltpu.make_async_copy(
                    array.at[pl.ds(index, count)],
                    right.at[
                        sectors + sector, (place[0] + side) % 2, pl.ds(slab, count), :, pl.ds(column, array.shape[2])
                    ],
                    sems.at[first + len(copies)],
                )
            )
            index += count
    return copies


def half_copy(half, distance, place, left, sem):
    slabs = lax.axis_size("slab")
    width = half.shape[3]
    slab = place[0] ^ distance
    column = pl.multiple_of(((slab % 2) * (slabs // 2) + slab // 2) * width, width)
    return pltpu.make_async_copy(half, left.at[:, :, :, pl.ds(column, width)], sem)


def gather_kernel(groups, nexts, unit, distances, cuts, place, basis, *refs):
    halves, refs = refs[: len(distances)], refs[len(distances) :]
    pairs, refs = [refs[2 * i : 2 * i + 2] for i in range(len(nexts))], refs[2 * len(nexts) :]
    left, *rights, sent, sems = refs
    copies = next_copies(nexts, place, [pair[0] for pair in pairs], 0, rights[0], sems, 0)
    copies += next_copies(nexts, place, [pair[1] for pair in pairs], 1, rights[0], sems, len(copies))
    for units, right in zip(groups, rights):
        copies += own_copies(units, unit, place, basis, right, sems, len(copies))
    for half, distance in zip(halves, distances):
        copies.append(half_copy(half, distance, place, left, sems.at[len(copies)]))
    for at, cut in enumerate(cuts):
        copies.append(pltpu.make_async_copy(pairs[-1][0].at[cut], sent.at[at], sems.at[len(copies)]))
    run(copies)


def gather(basis, groups, nexts, unit, pairs, halves, distances, cuts):
    sectors, depth, _ = basis.shape
    flavours, width = halves[0].shape[1:3]
    given = [in_vmem(array) for array in (basis, *halves, *(array for pair in pairs for array in pair))]
    copies = sum(map(len, groups)) * (depth // width) + 2 * sum(len(holds) for holds in nexts)
    shapes = [pltpu.VMEM((sectors, flavours, width, depth), jnp.bfloat16)]
    for units in groups:
        columns = sum(count for _, count in units) * unit
        shapes.append(pltpu.VMEM((2 * sectors, 2, depth // width // 2, width, columns), jnp.bfloat16))
    shapes.append(pltpu.VMEM((len(cuts), width, unit), jnp.bfloat16))
    return kernel_call(
        functools.partial(gather_kernel, groups, nexts, unit, distances, cuts),
        "gather",
        basis.shape[:2],
        given,
        [WHOLE] * len(given),
        shapes,
        [WHOLE] * len(shapes),
        [pltpu.SemaphoreType.DMA((copies + len(halves) + len(cuts),))],
    )


def product(place, partner, sector, flavour, left, right):
    index = (partner[...][sector, flavour] - place[1] + place[2]) % place[2]
    rows = right[index].reshape(left.shape[3], right.shape[4])
    return jnp.dot(left[sector, flavour], rows, preferred_element_type=jnp.float32).astype(jnp.bfloat16)


def early_kernel(distance, place, partner, half, right, _, left, stage, sem):
    run([half_copy(half, distance, place, left, sem)])
    sectors, flavours = left.shape[:2]
    for sector in range(sectors):
        for flavour in range(flavours):
            stage[flavour, sector] = product(place, partner, sector, flavour, left, right)


def early_products(partner, half, distance, left, right):
    sectors, flavours, width, _ = left.shape
    return kernel_call(
        functools.partial(early_kernel, distance),
        "early",
        (left.shape[0], left.shape[3]),
        [partner, in_vmem(half), in_vmem(right), in_vmem(left)],
        [WHOLE] + [WHOLE] * 3,
        [
            pltpu.VMEM(left.shape, left.dtype),
            pltpu.VMEM((flavours, sectors, width, right.shape[4]), jnp.bfloat16),
        ],
        [WHOLE] * 2,
        [pltpu.SemaphoreType.DMA],
        {3: 0},
    )


def partial(place, partner, sector, flavour, side, left, right):
    index = (partner[...][sector, flavour] - place[1] + place[2]) % place[2]
    core = (place[0] + side) % 2
    half = left.shape[3] // 2
    rows = right[index, core].reshape(half, right.shape[4])
    columns = pl.ds(pl.multiple_of(core * half, half), half)
    return jnp.dot(left[sector, flavour, :, columns], rows, preferred_element_type=jnp.float32)


def own_rows_kernel(groups, place, partner, left, *refs):
    arrays = []
    for nexts in groups:
        arrays.append(refs[: len(nexts)])
        refs = refs[len(nexts) :]
    refs = refs[len(groups) :]
    totals, rights, sems = refs[: len(groups)], refs[len(groups) : 2 * len(groups)], refs[2 * len(groups) :]
    copies = [
        next_copies(nexts, place, here, 0, right, sem, 0)
        for nexts, here, right, sem in zip(groups, arrays, rights, sems)
    ]
    for group in copies:
        for copy in group:
            copy.start()
    sectors, flavours = left.shape[:2]
    for group, total, right in zip(copies, totals, rights):
        for copy in group:
            copy.wait()
        for sector in range(sectors):
            for flavour in range(flavours):
                total[flavour, sector] = partial(place, partner, sector, flavour, 0, left, right)


def own_rows(partner, groups, arrays, left, rights):
    sectors, flavours, width, depth = left.shape
    given = [in_vmem(array) for array in (left, *(array for group in arrays for array in group), *rights)]
    first = 1 + len(given) - len(rights)
    return kernel_call(
        functools.partial(own_rows_kernel, groups),
        "own_rows",
        (sectors, depth),
        [partner, *given],
        [WHOLE] * (1 + len(given)),
        [pltpu.VMEM((flavours, sectors, width, right.shape[4]), jnp.float32) for right in rights]
        + [pltpu.VMEM(right.shape, right.dtype) for right in rights],
        [WHOLE] * (2 * len(rights)),
        [pltpu.SemaphoreType.DMA((sum(map(len, nexts)),)) for nexts in groups],
        {first + at: len(rights) + at for at in range(len(rights))},
    )


def late_kernel(earlier_units, units, nexts, unit, place, partner, left, total, *refs):
    earlier, refs = refs[: len(earlier_units)], refs[len(earlier_units) :]
    arrays, (_, out, right, stage, sems, early_sems, out_sems) = refs[: len(nexts)], refs[len(nexts) :]
    sectors, flavours = left.shape[:2]
    next_here = next_copies(nexts, place, arrays, 1, right, sems, 0)
    for copy in next_here:
        copy.start()
    out_copies = []
    for result, spans in zip(earlier, earlier_units):
        at = 0
        for start, count in spans:
            out_copies.append(
                pltpu.make_async_copy(
                    result.at[:, :, :, pl.ds(at, count * unit)],
                    out.at[:, :, :, pl.ds(first_column(start, place, unit), count * unit)],
                    early_sems.at[len(out_copies)],
                )
            )
            out_copies[-1].start()
            at += count * unit
    for copy in next_here:
        copy.wait()
    for sector in range(sectors):
        for flavour in range(flavours):
            rest = partial(place, partner, sector, flavour, 1, left, right)
            stage[flavour, sector] = (total[flavour, sector] + rest).astype(jnp.bfloat16)
            at = 0
            for number, (start, count) in enumerate(units):
                copy = pltpu.make_async_copy(
                    stage.at[flavour, sector, :, pl.ds(at, count * unit)],
                    out.at[flavour, sector, :, pl.ds(first_column(start, place, unit), count * unit)],
                    out_sems.at[sector * flavours + flavour, number],
                )
                copy.start()
                out_copies.append(copy)
                at += count * unit
    for copy in out_copies:
        copy.wait()


def late_products(partner, groups, nexts, unit, arrays, left, total, earlier, right):
    sectors, flavours, width, depth = left.shape
    given = [in_vmem(array) for array in (left, total, *earlier, *arrays, right)]
    return kernel_call(
        functools.partial(late_kernel, groups[:-1], groups[-1], nexts, unit),
        "late",
        (sectors, depth),
        [partner, *given],
        [WHOLE] * (1 + len(given)),
        [
            pltpu.HBM((flavours, sectors, width, depth), jnp.bfloat16),
            pltpu.VMEM(right.shape, right.dtype),
        ],
        [ANY, WHOLE],
        [
            pltpu.VMEM((flavours, sectors, width, right.shape[4]), jnp.bfloat16),
            pltpu.SemaphoreType.DMA((sum(map(len, nexts)),)),
            pltpu.SemaphoreType.DMA((sum(map(len, groups[:-1])),)),
            pltpu.SemaphoreType.DMA((sectors * flavours, len(groups[-1]))),
        ],
        {len(given): 1},
    )[0]


def local(basis, fermion, partner):
    sectors, depth, _ = basis.shape
    unit = depth // 8
    partner = partner.T
    distances = (3, 2, 1, 0)
    slabs = range(lax.axis_size("slab") // 2)
    held = [(sector, slab) for sector in range(sectors) for slab in slabs]
    alone = len(held) // 4
    count = 3
    units = ((0, count), (OWN, 1)), ((count, 6 - count), (OTHER, 1))
    first_blocks = [(sector, units[0], slab) for sector, slab in held]
    last_blocks = [(sector, ((start, 1),), slab) for start in range(count, 6) for sector, slab in held]
    last_blocks += [(sector, ((OTHER, 1),), slab) for sector, slab in held[:alone]]
    first_part, *far = basis_part(basis, fermion, first_blocks, unit, distances[:2])
    first = previous(first_part)
    far3, far2 = far_blocks(basis, fermion, distances[:2], far)
    got2, got3 = swapped(far2, 2), swapped(far3, 3)
    mine, near, last_part = near_blocks(basis, fermion, last_blocks, unit, distances[2:], far2)
    beside, last = swapped(mine, 1), previous(last_part)

    def runs(column, blocks):
        found = []
        for sector, slab in blocks:
            if found and found[-1][0] == sector:
                found[-1][2] += 1
            else:
                found.append([sector, slab, 1, column])
        return found

    groups = ((0, 2), (2, 4))
    every = slice(None)
    pieces = cut_out(first, [(every, every, slice(begin * unit, end * unit)) for begin, end in groups], (beside, got2))
    pairs = [(piece, swapped(piece, 1)) for piece in pieces]
    nexts = [runs(begin * unit, held) for begin, _ in groups]
    cuts = [(at, every, pl.ds((groups[-1][1] - groups[-1][0] - 1) * unit, unit)) for at in range(alone, len(held))]
    left, early_right, late_right, sent = gather(
        basis, units, nexts, unit, pairs, [got2, beside, near], distances[1:], cuts
    )
    other = swapped(sent, 2)
    left, early = early_products(partner, got3, distances[0], left, early_right)
    last, other, early = lax.optimization_barrier((last, other, early))
    last_other, other_other = swapped(last, 1), swapped(other, 1)
    nexts = [[], runs((6 - count) * unit, held[alone:])]
    for at in range(6 - count):
        nexts[0] += runs(at * unit, held)
    nexts[0] += runs((6 - count) * unit, held[:alone])
    total, late_right = own_rows(partner, [nexts], [[last, other]], left, [late_right])
    return late_products(
        partner, units, nexts, unit, [last_other, other_other], left, total, [early], late_right
    )


def solution(mesh):
    placed = (P("sec", None, None), P(None, "sec", None, "slab"), P(None, "sec"))
    return jax.shard_map(
        local, mesh=mesh, in_specs=placed, out_specs=P(None, "sec", "slab", None), check_vma=False
    )
```

```python
import functools

import jax
import jax.numpy as jnp
from jax import lax
from jax.experimental import pallas as pl
from jax.experimental.pallas import tpu as pltpu
from jax.sharding import PartitionSpec as P

ANY = pl.BlockSpec(memory_space=pl.ANY)
WHOLE = pl.BlockSpec(memory_space=pltpu.VMEM)
OWN, OTHER = -1, -2
KERNEL_BYTES = 16 * 1024 * 1024
BRIEF = pl.CostEstimate(flops=0, bytes_accessed=0, transcendentals=0)


def in_hbm(array):
    return pltpu.with_memory_space_constraint(array, pltpu.HBM)


def in_vmem(array):
    return pltpu.with_memory_space_constraint(array, pltpu.VMEM)


def located(sectors, depth):
    first = lax.axis_index("sec") * sectors
    return lax.axis_index("slab"), first, lax.axis_size("sec") * sectors, depth - depth // 8 * 2


def kernel_call(body, name, shape, given, specs, shapes, out_specs, scratch=(), aliases={}, cost=BRIEF):
    def kernel(*refs):
        body(*(() if shape is None else (located(*shape),)), *refs)

    return pl.pallas_call(
        kernel,
        out_shape=shapes,
        in_specs=specs,
        out_specs=out_specs,
        scratch_shapes=list(scratch),
        input_output_aliases=aliases,
        compiler_params=pltpu.CompilerParams(vmem_limit_bytes=KERNEL_BYTES),
        cost_estimate=cost,
        name=name,
    )(*given)


def first_column(unit, place, width):
    if unit == OWN:
        return pl.multiple_of(place[3] + (place[0] // 2) * width, width)
    if unit == OTHER:
        return pl.multiple_of(place[3] + (1 - place[0] // 2) * width, width)
    return unit * width


def run(copies):
    for copy in copies:
        copy.start()
    for copy in copies:
        copy.wait()


def previous(block):
    count = lax.axis_size("sec")
    return lax.ppermute(block, "sec", [((i + 1) % count, i) for i in range(count)])


def swapped(block, distance):
    return lax.ppermute(block, "slab", [(i, i ^ distance) for i in range(lax.axis_size("slab"))])


def part_copies(blocks, unit, place, basis, array, sems):
    rows = basis.shape[1] // lax.axis_size("slab")
    copies = []
    for at, (sector, spans, slab) in enumerate(blocks):
        row = pl.multiple_of((2 * slab + place[0] % 2) * rows, rows)
        column = 0
        for start, count in spans:
            copies.append(
                pltpu.make_async_copy(
                    basis.at[sector, pl.ds(row, rows), pl.ds(first_column(start, place, unit), count * unit)],
                    array.at[at, :, pl.ds(column, count * unit)],
                    sems.at[len(copies)],
                )
            )
            column += count * unit
    return copies


def part_shape(blocks, rows, unit):
    return pltpu.VMEM((len(blocks), rows, sum(count for _, count in blocks[0][1]) * unit), jnp.bfloat16)


def part_sems(blocks):
    return pltpu.SemaphoreType.DMA((sum(len(spans) for _, spans, _ in blocks),))


def half_products(sectors, distances, place, basis, fermion, pieces, ready=lambda sector: None):
    flavours, _, _, width = fermion.shape
    for sector in sectors:
        ready(sector)
        right = jnp.concatenate([fermion[flavour, sector] for flavour in range(flavours)], axis=1)
        for slot, distance in enumerate(distances):
            column = pl.multiple_of((place[0] ^ distance) * width, width)
            block = lax.dot_general(
                basis[sector, :, pl.ds(column, width)],
                right,
                (((0,), (0,)), ((), ())),
                preferred_element_type=jnp.float32,
            ).astype(jnp.bfloat16)
            for flavour in range(flavours):
                pieces[slot][sector, flavour] = block[:, flavour * width : (flavour + 1) * width]


def part_kernel(blocks, unit, distances, place, basis, fermion, sent, *refs):
    *pieces, left, right, sems, half_sems = refs
    copies = part_copies(blocks, unit, place, basis, sent, sems)
    for copy in copies:
        copy.start()

    @pl.when(place[1] == 0)
    def _():
        held = [
            [
                pltpu.make_async_copy(basis.at[sector], left.at[sector], half_sems.at[sector, 0]),
                pltpu.make_async_copy(fermion.at[:, sector], right.at[:, sector], half_sems.at[sector, 1]),
            ]
            for sector in range(basis.shape[0])
        ]
        for pair in held:
            for copy in pair:
                copy.start()

        def ready(sector):
            for copy in held[sector]:
                copy.wait()

        half_products(range(basis.shape[0]), distances, place, left, right, pieces, ready)

    for copy in copies:
        copy.wait()


def basis_part(basis, fermion, blocks, unit, distances):
    flavours, sectors, depth, width = fermion.shape
    shapes = [part_shape(blocks, width, unit)]
    shapes += [pltpu.VMEM((sectors, flavours, width, width), jnp.bfloat16)] * len(distances)
    return kernel_call(
        functools.partial(part_kernel, blocks, unit, distances),
        "part",
        basis.shape[:2],
        [in_hbm(basis), in_hbm(fermion)],
        [ANY, ANY],
        shapes,
        [WHOLE] * len(shapes),
        [
            pltpu.VMEM((sectors, depth, depth), jnp.bfloat16),
            pltpu.VMEM((flavours, sectors, depth, width), jnp.bfloat16),
            part_sems(blocks),
            pltpu.SemaphoreType.DMA((sectors, 2)),
        ],
    )


def far_kernel(distances, place, basis, fermion, *refs):
    pieces = refs[len(distances) :]

    @pl.when(place[1] != 0)
    def _():
        half_products(range(basis.shape[0]), distances, place, basis, fermion, pieces)


def far_blocks(basis, fermion, distances, earlier):
    return kernel_call(
        functools.partial(far_kernel, distances),
        "far",
        basis.shape[:2],
        [in_vmem(basis), in_vmem(fermion), *map(in_vmem, earlier)],
        [WHOLE] * (2 + len(earlier)),
        [pltpu.VMEM(piece.shape, piece.dtype) for piece in earlier],
        [WHOLE] * len(distances),
        aliases={2 + at: at for at in range(len(earlier))},
    )


def near_kernel(blocks, unit, distances, place, basis, fermion, _, *refs):
    *pieces, sent, sems = refs
    copies = part_copies(blocks, unit, place, basis, sent, sems)
    for copy in copies:
        copy.start()
    half_products(range(basis.shape[0]), distances, place, basis, fermion, pieces)
    for copy in copies:
        copy.wait()


def near_blocks(basis, fermion, blocks, unit, distances, after):
    flavours, sectors, depth, width = fermion.shape
    return kernel_call(
        functools.partial(near_kernel, blocks, unit, distances),
        "near",
        basis.shape[:2],
        [in_vmem(basis), in_vmem(fermion), in_vmem(after)],
        [WHOLE, WHOLE, WHOLE],
        [pltpu.VMEM((sectors, flavours, width, width), jnp.bfloat16)] * len(distances)
        + [part_shape(blocks, width, unit)],
        [WHOLE] * (len(distances) + 1),
        [part_sems(blocks)],
    )


def cut_kernel(cuts, given, *refs):
    for cut, piece in zip(cuts, refs[-len(cuts) :]):
        piece[...] = given[cut]


def cut_out(array, cuts, after=()):
    shapes = [jax.eval_shape(lambda x, cut=cut: x[cut], array).shape for cut in cuts]
    return kernel_call(
        functools.partial(cut_kernel, cuts),
        "cut",
        None,
        [in_vmem(array), *map(in_vmem, after)],
        [WHOLE] * (1 + len(after)),
        [pltpu.VMEM(shape, array.dtype) for shape in shapes],
        [WHOLE] * len(cuts),
    )


def own_copies(units, unit, place, basis, right, sems, first):
    sectors, depth, _ = basis.shape
    slabs = lax.axis_size("slab")
    rows = depth // slabs
    copies, at = [], 0
    for start, count in units:
        for slab in range(slabs):
            copies.append(
                pltpu.make_async_copy(
                    basis.at[:, pl.ds(slab * rows, rows), pl.ds(first_column(start, place, unit), count * unit)],
                    right.at[pl.ds(0, sectors), slab % 2, slab // 2, :, pl.ds(at, count * unit)],
                    sems.at[first + len(copies)],
                )
            )
        at += count * unit
    return copies


def next_copies(nexts, place, arrays, side, right, sems, first):
    sectors = right.shape[0] // 2
    copies = []
    for array, runs in zip(arrays, nexts):
        index = 0
        for sector, slab, count, column in runs:
            copies.append(
                pltpu.make_async_copy(
                    array.at[pl.ds(index, count)],
                    right.at[
                        sectors + sector, (place[0] + side) % 2, pl.ds(slab, count), :, pl.ds(column, array.shape[2])
                    ],
                    sems.at[first + len(copies)],
                )
            )
            index += count
    return copies


def half_copy(half, distance, place, left, sem):
    slabs = lax.axis_size("slab")
    width = half.shape[3]
    slab = place[0] ^ distance
    column = pl.multiple_of(((slab % 2) * (slabs // 2) + slab // 2) * width, width)
    return pltpu.make_async_copy(half, left.at[:, :, :, pl.ds(column, width)], sem)


def gather_kernel(groups, nexts, unit, distances, cuts, place, basis, *refs):
    halves, refs = refs[: len(distances)], refs[len(distances) :]
    pairs, refs = [refs[2 * i : 2 * i + 2] for i in range(len(nexts))], refs[2 * len(nexts) :]
    left, *rights, sent, sems = refs
    copies = next_copies(nexts, place, [pair[0] for pair in pairs], 0, rights[0], sems, 0)
    copies += next_copies(nexts, place, [pair[1] for pair in pairs], 1, rights[0], sems, len(copies))
    for units, right in zip(groups, rights):
        copies += own_copies(units, unit, place, basis, right, sems, len(copies))
    for half, distance in zip(halves, distances):
        copies.append(half_copy(half, distance, place, left, sems.at[len(copies)]))
    for at, cut in enumerate(cuts):
        copies.append(pltpu.make_async_copy(pairs[-1][0].at[cut], sent.at[at], sems.at[len(copies)]))
    run(copies)


def gather(basis, groups, nexts, unit, pairs, halves, distances, cuts):
    sectors, depth, _ = basis.shape
    flavours, width = halves[0].shape[1:3]
    given = [in_vmem(array) for array in (basis, *halves, *(array for pair in pairs for array in pair))]
    copies = sum(map(len, groups)) * (depth // width) + 2 * sum(len(holds) for holds in nexts)
    shapes = [pltpu.VMEM((sectors, flavours, width, depth), jnp.bfloat16)]
    for units in groups:
        columns = sum(count for _, count in units) * unit
        shapes.append(pltpu.VMEM((2 * sectors, 2, depth // width // 2, width, columns), jnp.bfloat16))
    shapes.append(pltpu.VMEM((len(cuts), width, unit), jnp.bfloat16))
    return kernel_call(
        functools.partial(gather_kernel, groups, nexts, unit, distances, cuts),
        "gather",
        basis.shape[:2],
        given,
        [WHOLE] * len(given),
        shapes,
        [WHOLE] * len(shapes),
        [pltpu.SemaphoreType.DMA((copies + len(halves) + len(cuts),))],
    )


def product(place, partner, sector, flavour, left, right):
    index = (partner[...][sector, flavour] - place[1] + place[2]) % place[2]
    rows = right[index].reshape(left.shape[3], right.shape[4])
    return jnp.dot(left[sector, flavour], rows, preferred_element_type=jnp.float32).astype(jnp.bfloat16)


def early_kernel(distance, place, partner, half, right, _, left, stage, sem):
    run([half_copy(half, distance, place, left, sem)])
    sectors, flavours = left.shape[:2]
    for sector in range(sectors):
        for flavour in range(flavours):
            stage[flavour, sector] = product(place, partner, sector, flavour, left, right)


def early_products(partner, half, distance, left, right):
    sectors, flavours, width, _ = left.shape
    return kernel_call(
        functools.partial(early_kernel, distance),
        "early",
        (left.shape[0], left.shape[3]),
        [partner, in_vmem(half), in_vmem(right), in_vmem(left)],
        [WHOLE] + [WHOLE] * 3,
        [
            pltpu.VMEM(left.shape, left.dtype),
            pltpu.VMEM((flavours, sectors, width, right.shape[4]), jnp.bfloat16),
        ],
        [WHOLE] * 2,
        [pltpu.SemaphoreType.DMA],
        {3: 0},
    )


def partial(place, partner, sector, flavour, side, left, right):
    index = (partner[...][sector, flavour] - place[1] + place[2]) % place[2]
    core = (place[0] + side) % 2
    half = left.shape[3] // 2
    rows = right[index, core].reshape(half, right.shape[4])
    columns = pl.ds(pl.multiple_of(core * half, half), half)
    return jnp.dot(left[sector, flavour, :, columns], rows, preferred_element_type=jnp.float32)


def own_rows_kernel(groups, place, partner, left, *refs):
    arrays = []
    for nexts in groups:
        arrays.append(refs[: len(nexts)])
        refs = refs[len(nexts) :]
    refs = refs[len(groups) :]
    totals, rights, sems = refs[: len(groups)], refs[len(groups) : 2 * len(groups)], refs[2 * len(groups) :]
    copies = [
        next_copies(nexts, place, here, 0, right, sem, 0)
        for nexts, here, right, sem in zip(groups, arrays, rights, sems)
    ]
    for group in copies:
        for copy in group:
            copy.start()
    sectors, flavours = left.shape[:2]
    for group, total, right in zip(copies, totals, rights):
        for copy in group:
            copy.wait()
        for sector in range(sectors):
            for flavour in range(flavours):
                total[flavour, sector] = partial(place, partner, sector, flavour, 0, left, right)


def own_rows(partner, groups, arrays, left, rights):
    sectors, flavours, width, depth = left.shape
    given = [in_vmem(array) for array in (left, *(array for group in arrays for array in group), *rights)]
    first = 1 + len(given) - len(rights)
    return kernel_call(
        functools.partial(own_rows_kernel, groups),
        "own_rows",
        (sectors, depth),
        [partner, *given],
        [WHOLE] * (1 + len(given)),
        [pltpu.VMEM((flavours, sectors, width, right.shape[4]), jnp.float32) for right in rights]
        + [pltpu.VMEM(right.shape, right.dtype) for right in rights],
        [WHOLE] * (2 * len(rights)),
        [pltpu.SemaphoreType.DMA((sum(map(len, nexts)),)) for nexts in groups],
        {first + at: len(rights) + at for at in range(len(rights))},
    )


def late_kernel(earlier_units, units, nexts, unit, place, partner, left, total, *refs):
    earlier, refs = refs[: len(earlier_units)], refs[len(earlier_units) :]
    arrays, (_, out, right, stage, sems, early_sems, out_sems) = refs[: len(nexts)], refs[len(nexts) :]
    sectors, flavours = left.shape[:2]
    next_here = next_copies(nexts, place, arrays, 1, right, sems, 0)
    for copy in next_here:
        copy.start()
    out_copies = []
    for result, spans in zip(earlier, earlier_units):
        at = 0
        for start, count in spans:
            out_copies.append(
                pltpu.make_async_copy(
                    result.at[:, :, :, pl.ds(at, count * unit)],
                    out.at[:, :, :, pl.ds(first_column(start, place, unit), count * unit)],
                    early_sems.at[len(out_copies)],
                )
            )
            out_copies[-1].start()
            at += count * unit
    for copy in next_here:
        copy.wait()
    for sector in range(sectors):
        for flavour in range(flavours):
            rest = partial(place, partner, sector, flavour, 1, left, right)
            stage[flavour, sector] = (total[flavour, sector] + rest).astype(jnp.bfloat16)
            at = 0
            for number, (start, count) in enumerate(units):
                copy = pltpu.make_async_copy(
                    stage.at[flavour, sector, :, pl.ds(at, count * unit)],
                    out.at[flavour, sector, :, pl.ds(first_column(start, place, unit), count * unit)],
                    out_sems.at[sector * flavours + flavour, number],
                )
                copy.start()
                out_copies.append(copy)
                at += count * unit
    for copy in out_copies:
        copy.wait()


def late_products(partner, groups, nexts, unit, arrays, left, total, earlier, right):
    sectors, flavours, width, depth = left.shape
    given = [in_vmem(array) for array in (left, total, *earlier, *arrays, right)]
    return kernel_call(
        functools.partial(late_kernel, groups[:-1], groups[-1], nexts, unit),
        "late",
        (sectors, depth),
        [partner, *given],
        [WHOLE] * (1 + len(given)),
        [
            pltpu.HBM((flavours, sectors, width, depth), jnp.bfloat16),
            pltpu.VMEM(right.shape, right.dtype),
        ],
        [ANY, WHOLE],
        [
            pltpu.VMEM((flavours, sectors, width, right.shape[4]), jnp.bfloat16),
            pltpu.SemaphoreType.DMA((sum(map(len, nexts)),)),
            pltpu.SemaphoreType.DMA((sum(map(len, groups[:-1])),)),
            pltpu.SemaphoreType.DMA((sectors * flavours, len(groups[-1]))),
        ],
        {len(given): 1},
    )[0]


def local(basis, fermion, partner):
    sectors, depth, _ = basis.shape
    unit = depth // 8
    partner = partner.T
    distances = tuple(reversed(range(lax.axis_size("slab"))))
    slabs = range(lax.axis_size("slab") // 2)
    held = [(sector, slab) for sector in range(sectors) for slab in slabs]
    alone = len(held) // 4
    count = 3
    units = ((0, count), (OWN, 1)), ((count, 6 - count), (OTHER, 1))
    first_blocks = [(sector, units[0], slab) for sector, slab in held]
    last_blocks = [(sector, ((start, 1),), slab) for start in range(count, 6) for sector, slab in held]
    last_blocks += [(sector, ((OTHER, 1),), slab) for sector, slab in held[:alone]]
    first_part, *far = basis_part(basis, fermion, first_blocks, unit, distances[:2])
    first = previous(first_part)
    far3, far2 = far_blocks(basis, fermion, distances[:2], far)
    got3, got2 = swapped(far3, distances[0]), swapped(far2, distances[1])
    mine, near, last_part = near_blocks(basis, fermion, last_blocks, unit, distances[2:], far2)
    beside, last = swapped(mine, distances[2]), previous(last_part)

    def runs(column, blocks):
        found = []
        for sector, slab in blocks:
            if found and found[-1][0] == sector:
                found[-1][2] += 1
            else:
                found.append([sector, slab, 1, column])
        return found

    groups = ((0, 2), (2, 4))
    every = slice(None)
    pieces = cut_out(first, [(every, every, slice(begin * unit, end * unit)) for begin, end in groups], (beside, got2))
    pairs = [(piece, swapped(piece, 1)) for piece in pieces]
    nexts = [runs(begin * unit, held) for begin, _ in groups]
    cuts = [(at, every, pl.ds((groups[-1][1] - groups[-1][0] - 1) * unit, unit)) for at in range(alone, len(held))]
    left, early_right, late_right, sent = gather(
        basis, units, nexts, unit, pairs, [got2, beside, near], distances[1:], cuts
    )
    other = swapped(sent, distances[1])
    left, early = early_products(partner, got3, distances[0], left, early_right)
    last, other, early = lax.optimization_barrier((last, other, early))
    last_other, other_other = swapped(last, 1), swapped(other, 1)
    nexts = [[], runs((6 - count) * unit, held[alone:])]
    for at in range(6 - count):
        nexts[0] += runs(at * unit, held)
    nexts[0] += runs((6 - count) * unit, held[:alone])
    total, late_right = own_rows(partner, [nexts], [[last, other]], left, [late_right])
    return late_products(
        partner, units, nexts, unit, [last_other, other_other], left, total, [early], late_right
    )


def solution(mesh):
    placed = (P("sec", None, None), P(None, "sec", None, "slab"), P(None, "sec"))
    return jax.shard_map(
        local, mesh=mesh, in_specs=placed, out_specs=P(None, "sec", "slab", None), check_vma=False
    )
```

```python
import functools

import jax
import jax.numpy as jnp
from jax import lax
from jax.experimental import pallas as pl
from jax.experimental.pallas import tpu as pltpu
from jax.sharding import PartitionSpec as P

ANY = pl.BlockSpec(memory_space=pl.ANY)
WHOLE = pl.BlockSpec(memory_space=pltpu.VMEM)
OWN, OTHER = -1, -2
KERNEL_BYTES = 16 * 1024 * 1024
BRIEF = pl.CostEstimate(flops=0, bytes_accessed=0, transcendentals=0)


def in_hbm(array):
    return pltpu.with_memory_space_constraint(array, pltpu.HBM)


def in_vmem(array):
    return pltpu.with_memory_space_constraint(array, pltpu.VMEM)


def located(sectors, depth):
    first = lax.axis_index("sec") * sectors
    return lax.axis_index("slab"), first, lax.axis_size("sec") * sectors, depth - depth // 8 * 2


def kernel_call(body, name, shape, given, specs, shapes, out_specs, scratch=(), aliases={}, cost=BRIEF):
    def kernel(*refs):
        body(*(() if shape is None else (located(*shape),)), *refs)

    return pl.pallas_call(
        kernel,
        out_shape=shapes,
        in_specs=specs,
        out_specs=out_specs,
        scratch_shapes=list(scratch),
        input_output_aliases=aliases,
        compiler_params=pltpu.CompilerParams(vmem_limit_bytes=KERNEL_BYTES),
        cost_estimate=cost,
        name=name,
    )(*given)


def first_column(unit, place, width):
    if unit == OWN:
        return pl.multiple_of(place[3] + (place[0] // 2) * width, width)
    if unit == OTHER:
        return pl.multiple_of(place[3] + (1 - place[0] // 2) * width, width)
    return unit * width


def run(copies):
    for copy in copies:
        copy.start()
    for copy in copies:
        copy.wait()


def previous(block):
    count = lax.axis_size("sec")
    return lax.ppermute(block, "sec", [((i + 1) % count, i) for i in range(count)])


def swapped(block, distance):
    return lax.ppermute(block, "slab", [(i, i ^ distance) for i in range(lax.axis_size("slab"))])


def part_copies(blocks, unit, place, basis, array, sems):
    rows = basis.shape[1] // lax.axis_size("slab")
    copies = []
    for at, (sector, spans, slab) in enumerate(blocks):
        row = pl.multiple_of((2 * slab + place[0] % 2) * rows, rows)
        column = 0
        for start, count in spans:
            copies.append(
                pltpu.make_async_copy(
                    basis.at[sector, pl.ds(row, rows), pl.ds(first_column(start, place, unit), count * unit)],
                    array.at[at, :, pl.ds(column, count * unit)],
                    sems.at[len(copies)],
                )
            )
            column += count * unit
    return copies


def part_shape(blocks, rows, unit):
    return pltpu.VMEM((len(blocks), rows, sum(count for _, count in blocks[0][1]) * unit), jnp.bfloat16)


def part_sems(blocks):
    return pltpu.SemaphoreType.DMA((sum(len(spans) for _, spans, _ in blocks),))


def half_products(sectors, distances, place, basis, fermion, pieces, ready=lambda sector: None, slots=None):
    flavours, _, _, width = fermion.shape
    for sector in sectors:
        ready(sector)
        right = jnp.concatenate([fermion[flavour, sector] for flavour in range(flavours)], axis=1)
        for slot, distance in enumerate(distances):
            column = slots[slot] if slots else pl.multiple_of((place[0] ^ distance) * width, width)
            block = lax.dot_general(
                basis[sector, :, pl.ds(column, width)],
                right,
                (((0,), (0,)), ((), ())),
                preferred_element_type=jnp.float32,
            ).astype(jnp.bfloat16)
            for flavour in range(flavours):
                pieces[slot][sector, flavour] = block[:, flavour * width : (flavour + 1) * width]


def part_kernel(blocks, unit, distances, place, basis, fermion, sent, *refs):
    *pieces, left, right, sems, half_sems = refs
    width = fermion.shape[3]
    copies = part_copies(blocks, unit, place, basis, sent, sems)
    for copy in copies:
        copy.start()

    @pl.when(place[1] == 0)
    def _():
        held = [
            [
                pltpu.make_async_copy(fermion.at[:, sector], right.at[:, sector], half_sems.at[sector, 0]),
                *(
                    pltpu.make_async_copy(
                        basis.at[sector, :, pl.ds(pl.multiple_of((place[0] ^ distance) * width, width), width)],
                        left.at[sector, :, pl.ds(slot * width, width)],
                        half_sems.at[sector, 1 + slot],
                    )
                    for slot, distance in enumerate(distances)
                ),
            ]
            for sector in range(basis.shape[0])
        ]
        for pair in held:
            for copy in pair:
                copy.start()

        def ready(sector):
            for copy in held[sector]:
                copy.wait()

        slots = [slot * width for slot in range(len(distances))]
        half_products(range(basis.shape[0]), distances, place, left, right, pieces, ready, slots)

    for copy in copies:
        copy.wait()


def basis_part(basis, fermion, blocks, unit, distances):
    flavours, sectors, depth, width = fermion.shape
    shapes = [part_shape(blocks, width, unit)]
    shapes += [pltpu.VMEM((sectors, flavours, width, width), jnp.bfloat16)] * len(distances)
    return kernel_call(
        functools.partial(part_kernel, blocks, unit, distances),
        "part",
        basis.shape[:2],
        [in_hbm(basis), in_hbm(fermion)],
        [ANY, ANY],
        shapes,
        [WHOLE] * len(shapes),
        [
            pltpu.VMEM((sectors, depth, len(distances) * width), jnp.bfloat16),
            pltpu.VMEM((flavours, sectors, depth, width), jnp.bfloat16),
            part_sems(blocks),
            pltpu.SemaphoreType.DMA((sectors, 1 + len(distances))),
        ],
    )


def far_kernel(distances, place, basis, fermion, *refs):
    pieces = refs[len(distances) :]

    @pl.when(place[1] != 0)
    def _():
        half_products(range(basis.shape[0]), distances, place, basis, fermion, pieces)


def far_blocks(basis, fermion, distances, earlier):
    return kernel_call(
        functools.partial(far_kernel, distances),
        "far",
        basis.shape[:2],
        [in_vmem(basis), in_vmem(fermion), *map(in_vmem, earlier)],
        [WHOLE] * (2 + len(earlier)),
        [pltpu.VMEM(piece.shape, piece.dtype) for piece in earlier],
        [WHOLE] * len(distances),
        aliases={2 + at: at for at in range(len(earlier))},
    )


def near_kernel(blocks, unit, distances, place, basis, fermion, _, *refs):
    *pieces, sent, sems = refs
    copies = part_copies(blocks, unit, place, basis, sent, sems)
    for copy in copies:
        copy.start()
    half_products(range(basis.shape[0]), distances, place, basis, fermion, pieces)
    for copy in copies:
        copy.wait()


def near_blocks(basis, fermion, blocks, unit, distances, after):
    flavours, sectors, depth, width = fermion.shape
    return kernel_call(
        functools.partial(near_kernel, blocks, unit, distances),
        "near",
        basis.shape[:2],
        [in_vmem(basis), in_vmem(fermion), in_vmem(after)],
        [WHOLE, WHOLE, WHOLE],
        [pltpu.VMEM((sectors, flavours, width, width), jnp.bfloat16)] * len(distances)
        + [part_shape(blocks, width, unit)],
        [WHOLE] * (len(distances) + 1),
        [part_sems(blocks)],
    )


def cut_kernel(cuts, given, *refs):
    for cut, piece in zip(cuts, refs[-len(cuts) :]):
        piece[...] = given[cut]


def cut_out(array, cuts, after=()):
    shapes = [jax.eval_shape(lambda x, cut=cut: x[cut], array).shape for cut in cuts]
    return kernel_call(
        functools.partial(cut_kernel, cuts),
        "cut",
        None,
        [in_vmem(array), *map(in_vmem, after)],
        [WHOLE] * (1 + len(after)),
        [pltpu.VMEM(shape, array.dtype) for shape in shapes],
        [WHOLE] * len(cuts),
    )


def own_copies(units, unit, place, basis, right, sems, first):
    sectors, depth, _ = basis.shape
    slabs = lax.axis_size("slab")
    rows = depth // slabs
    copies, at = [], 0
    for start, count in units:
        for slab in range(slabs):
            copies.append(
                pltpu.make_async_copy(
                    basis.at[:, pl.ds(slab * rows, rows), pl.ds(first_column(start, place, unit), count * unit)],
                    right.at[pl.ds(0, sectors), slab % 2, slab // 2, :, pl.ds(at, count * unit)],
                    sems.at[first + len(copies)],
                )
            )
        at += count * unit
    return copies


def next_copies(nexts, place, arrays, side, right, sems, first):
    sectors = right.shape[0] // 2
    copies = []
    for array, runs in zip(arrays, nexts):
        index = 0
        for sector, slab, count, column in runs:
            copies.append(
                pltpu.make_async_copy(
                    array.at[pl.ds(index, count)],
                    right.at[
                        sectors + sector, (place[0] + side) % 2, pl.ds(slab, count), :, pl.ds(column, array.shape[2])
                    ],
                    sems.at[first + len(copies)],
                )
            )
            index += count
    return copies


def half_copy(half, distance, place, left, sem):
    slabs = lax.axis_size("slab")
    width = half.shape[3]
    slab = place[0] ^ distance
    column = pl.multiple_of(((slab % 2) * (slabs // 2) + slab // 2) * width, width)
    return pltpu.make_async_copy(half, left.at[:, :, :, pl.ds(column, width)], sem)


def gather_kernel(groups, nexts, unit, distances, cuts, place, basis, *refs):
    halves, refs = refs[: len(distances)], refs[len(distances) :]
    pairs, refs = [refs[2 * i : 2 * i + 2] for i in range(len(nexts))], refs[2 * len(nexts) :]
    left, *rights, sent, sems = refs
    copies = next_copies(nexts, place, [pair[0] for pair in pairs], 0, rights[0], sems, 0)
    copies += next_copies(nexts, place, [pair[1] for pair in pairs], 1, rights[0], sems, len(copies))
    for units, right in zip(groups, rights):
        copies += own_copies(units, unit, place, basis, right, sems, len(copies))
    for half, distance in zip(halves, distances):
        copies.append(half_copy(half, distance, place, left, sems.at[len(copies)]))
    for at, cut in enumerate(cuts):
        copies.append(pltpu.make_async_copy(pairs[-1][0].at[cut], sent.at[at], sems.at[len(copies)]))
    run(copies)


def gather(basis, groups, nexts, unit, pairs, halves, distances, cuts):
    sectors, depth, _ = basis.shape
    flavours, width = halves[0].shape[1:3]
    given = [in_vmem(array) for array in (basis, *halves, *(array for pair in pairs for array in pair))]
    copies = sum(map(len, groups)) * (depth // width) + 2 * sum(len(holds) for holds in nexts)
    shapes = [pltpu.VMEM((sectors, flavours, width, depth), jnp.bfloat16)]
    for units in groups:
        columns = sum(count for _, count in units) * unit
        shapes.append(pltpu.VMEM((2 * sectors, 2, depth // width // 2, width, columns), jnp.bfloat16))
    shapes.append(pltpu.VMEM((len(cuts), width, unit), jnp.bfloat16))
    return kernel_call(
        functools.partial(gather_kernel, groups, nexts, unit, distances, cuts),
        "gather",
        basis.shape[:2],
        given,
        [WHOLE] * len(given),
        shapes,
        [WHOLE] * len(shapes),
        [pltpu.SemaphoreType.DMA((copies + len(halves) + len(cuts),))],
    )


def product(place, partner, sector, flavour, left, right):
    index = (partner[...][sector, flavour] - place[1] + place[2]) % place[2]
    rows = right[index].reshape(left.shape[3], right.shape[4])
    return jnp.dot(left[sector, flavour], rows, preferred_element_type=jnp.float32).astype(jnp.bfloat16)


def early_kernel(distance, place, partner, half, right, _, left, stage, sem):
    run([half_copy(half, distance, place, left, sem)])
    sectors, flavours = left.shape[:2]
    for sector in range(sectors):
        for flavour in range(flavours):
            stage[flavour, sector] = product(place, partner, sector, flavour, left, right)


def early_products(partner, half, distance, left, right):
    sectors, flavours, width, _ = left.shape
    return kernel_call(
        functools.partial(early_kernel, distance),
        "early",
        (left.shape[0], left.shape[3]),
        [partner, in_vmem(half), in_vmem(right), in_vmem(left)],
        [WHOLE] + [WHOLE] * 3,
        [
            pltpu.VMEM(left.shape, left.dtype),
            pltpu.VMEM((flavours, sectors, width, right.shape[4]), jnp.bfloat16),
        ],
        [WHOLE] * 2,
        [pltpu.SemaphoreType.DMA],
        {3: 0},
    )


def partial(place, partner, sector, flavour, side, left, right):
    index = (partner[...][sector, flavour] - place[1] + place[2]) % place[2]
    core = (place[0] + side) % 2
    half = left.shape[3] // 2
    rows = right[index, core].reshape(half, right.shape[4])
    columns = pl.ds(pl.multiple_of(core * half, half), half)
    return jnp.dot(left[sector, flavour, :, columns], rows, preferred_element_type=jnp.float32)


def own_rows_kernel(groups, place, partner, left, *refs):
    arrays = []
    for nexts in groups:
        arrays.append(refs[: len(nexts)])
        refs = refs[len(nexts) :]
    refs = refs[len(groups) :]
    totals, rights, sems = refs[: len(groups)], refs[len(groups) : 2 * len(groups)], refs[2 * len(groups) :]
    copies = [
        next_copies(nexts, place, here, 0, right, sem, 0)
        for nexts, here, right, sem in zip(groups, arrays, rights, sems)
    ]
    for group in copies:
        for copy in group:
            copy.start()
    sectors, flavours = left.shape[:2]
    for group, total, right in zip(copies, totals, rights):
        for copy in group:
            copy.wait()
        for sector in range(sectors):
            for flavour in range(flavours):
                total[flavour, sector] = partial(place, partner, sector, flavour, 0, left, right)


def own_rows(partner, groups, arrays, left, rights):
    sectors, flavours, width, depth = left.shape
    given = [in_vmem(array) for array in (left, *(array for group in arrays for array in group), *rights)]
    first = 1 + len(given) - len(rights)
    return kernel_call(
        functools.partial(own_rows_kernel, groups),
        "own_rows",
        (sectors, depth),
        [partner, *given],
        [WHOLE] * (1 + len(given)),
        [pltpu.VMEM((flavours, sectors, width, right.shape[4]), jnp.float32) for right in rights]
        + [pltpu.VMEM(right.shape, right.dtype) for right in rights],
        [WHOLE] * (2 * len(rights)),
        [pltpu.SemaphoreType.DMA((sum(map(len, nexts)),)) for nexts in groups],
        {first + at: len(rights) + at for at in range(len(rights))},
    )


def late_kernel(earlier_units, units, nexts, unit, place, partner, left, total, *refs):
    earlier, refs = refs[: len(earlier_units)], refs[len(earlier_units) :]
    arrays, (_, out, right, stage, sems, early_sems, out_sems) = refs[: len(nexts)], refs[len(nexts) :]
    sectors, flavours = left.shape[:2]
    next_here = next_copies(nexts, place, arrays, 1, right, sems, 0)
    for copy in next_here:
        copy.start()
    out_copies = []
    for result, spans in zip(earlier, earlier_units):
        at = 0
        for start, count in spans:
            out_copies.append(
                pltpu.make_async_copy(
                    result.at[:, :, :, pl.ds(at, count * unit)],
                    out.at[:, :, :, pl.ds(first_column(start, place, unit), count * unit)],
                    early_sems.at[len(out_copies)],
                )
            )
            out_copies[-1].start()
            at += count * unit
    for copy in next_here:
        copy.wait()
    for sector in range(sectors):
        for flavour in range(flavours):
            rest = partial(place, partner, sector, flavour, 1, left, right)
            stage[flavour, sector] = (total[flavour, sector] + rest).astype(jnp.bfloat16)
            at = 0
            for number, (start, count) in enumerate(units):
                copy = pltpu.make_async_copy(
                    stage.at[flavour, sector, :, pl.ds(at, count * unit)],
                    out.at[flavour, sector, :, pl.ds(first_column(start, place, unit), count * unit)],
                    out_sems.at[sector * flavours + flavour, number],
                )
                copy.start()
                out_copies.append(copy)
                at += count * unit
    for copy in out_copies:
        copy.wait()


def late_products(partner, groups, nexts, unit, arrays, left, total, earlier, right):
    sectors, flavours, width, depth = left.shape
    given = [in_vmem(array) for array in (left, total, *earlier, *arrays, right)]
    return kernel_call(
        functools.partial(late_kernel, groups[:-1], groups[-1], nexts, unit),
        "late",
        (sectors, depth),
        [partner, *given],
        [WHOLE] * (1 + len(given)),
        [
            pltpu.HBM((flavours, sectors, width, depth), jnp.bfloat16),
            pltpu.VMEM(right.shape, right.dtype),
        ],
        [ANY, WHOLE],
        [
            pltpu.VMEM((flavours, sectors, width, right.shape[4]), jnp.bfloat16),
            pltpu.SemaphoreType.DMA((sum(map(len, nexts)),)),
            pltpu.SemaphoreType.DMA((sum(map(len, groups[:-1])),)),
            pltpu.SemaphoreType.DMA((sectors * flavours, len(groups[-1]))),
        ],
        {len(given): 1},
    )[0]


def local(basis, fermion, partner):
    sectors, depth, _ = basis.shape
    unit = depth // 8
    partner = partner.T
    distances = tuple(reversed(range(lax.axis_size("slab"))))
    slabs = range(lax.axis_size("slab") // 2)
    held = [(sector, slab) for sector in range(sectors) for slab in slabs]
    alone = len(held) // 4
    count = 3
    units = ((0, count), (OWN, 1)), ((count, 6 - count), (OTHER, 1))
    first_blocks = [(sector, units[0], slab) for sector, slab in held]
    last_blocks = [(sector, ((start, 1),), slab) for start in range(count, 6) for sector, slab in held]
    last_blocks += [(sector, ((OTHER, 1),), slab) for sector, slab in held[:alone]]
    first_part, *far = basis_part(basis, fermion, first_blocks, unit, distances[:2])
    first = previous(first_part)
    far3, far2 = far_blocks(basis, fermion, distances[:2], far)
    got3, got2 = swapped(far3, distances[0]), swapped(far2, distances[1])
    mine, near, last_part = near_blocks(basis, fermion, last_blocks, unit, distances[2:], far2)
    beside, last = swapped(mine, distances[2]), previous(last_part)

    def runs(column, blocks):
        found = []
        for sector, slab in blocks:
            if found and found[-1][0] == sector:
                found[-1][2] += 1
            else:
                found.append([sector, slab, 1, column])
        return found

    groups = ((0, 2), (2, 4))
    every = slice(None)
    pieces = cut_out(first, [(every, every, slice(begin * unit, end * unit)) for begin, end in groups], (beside, got2))
    pairs = [(piece, swapped(piece, 1)) for piece in pieces]
    nexts = [runs(begin * unit, held) for begin, _ in groups]
    cuts = [(at, every, pl.ds((groups[-1][1] - groups[-1][0] - 1) * unit, unit)) for at in range(alone, len(held))]
    left, early_right, late_right, sent = gather(
        basis, units, nexts, unit, pairs, [got2, beside, near], distances[1:], cuts
    )
    other = swapped(sent, distances[1])
    left, early = early_products(partner, got3, distances[0], left, early_right)
    last, other, early = lax.optimization_barrier((last, other, early))
    last_other, other_other = swapped(last, 1), swapped(other, 1)
    nexts = [[], runs((6 - count) * unit, held[alone:])]
    for at in range(6 - count):
        nexts[0] += runs(at * unit, held)
    nexts[0] += runs((6 - count) * unit, held[:alone])
    total, late_right = own_rows(partner, [nexts], [[last, other]], left, [late_right])
    return late_products(
        partner, units, nexts, unit, [last_other, other_other], left, total, [early], late_right
    )


def solution(mesh):
    placed = (P("sec", None, None), P(None, "sec", None, "slab"), P(None, "sec"))
    return jax.shard_map(
        local, mesh=mesh, in_specs=placed, out_specs=P(None, "sec", "slab", None), check_vma=False
    )
```

```python
import functools

import jax
import jax.numpy as jnp
from jax import lax
from jax.experimental import pallas as pl
from jax.experimental.pallas import tpu as pltpu
from jax.sharding import PartitionSpec as P

ANY = pl.BlockSpec(memory_space=pl.ANY)
WHOLE = pl.BlockSpec(memory_space=pltpu.VMEM)
OWN, OTHER = -1, -2
KERNEL_BYTES = 16 * 1024 * 1024
BRIEF = pl.CostEstimate(flops=0, bytes_accessed=0, transcendentals=0)


def in_hbm(array):
    return pltpu.with_memory_space_constraint(array, pltpu.HBM)


def in_vmem(array):
    return pltpu.with_memory_space_constraint(array, pltpu.VMEM)


def located(sectors, depth):
    first = lax.axis_index("sec") * sectors
    return lax.axis_index("slab"), first, lax.axis_size("sec") * sectors, depth - depth // 8 * 2


def kernel_call(body, name, shape, given, specs, shapes, out_specs, scratch=(), aliases={}, cost=BRIEF):
    def kernel(*refs):
        body(*(() if shape is None else (located(*shape),)), *refs)

    return pl.pallas_call(
        kernel,
        out_shape=shapes,
        in_specs=specs,
        out_specs=out_specs,
        scratch_shapes=list(scratch),
        input_output_aliases=aliases,
        compiler_params=pltpu.CompilerParams(vmem_limit_bytes=KERNEL_BYTES),
        cost_estimate=cost,
        name=name,
    )(*given)


def first_column(unit, place, width):
    if unit == OWN:
        return pl.multiple_of(place[3] + (place[0] // 2) * width, width)
    if unit == OTHER:
        return pl.multiple_of(place[3] + (1 - place[0] // 2) * width, width)
    return unit * width


def run(copies):
    for copy in copies:
        copy.start()
    for copy in copies:
        copy.wait()


def previous(block):
    count = lax.axis_size("sec")
    return lax.ppermute(block, "sec", [((i + 1) % count, i) for i in range(count)])


def swapped(block, distance):
    return lax.ppermute(block, "slab", [(i, i ^ distance) for i in range(lax.axis_size("slab"))])


def part_copies(blocks, unit, place, basis, array, sems):
    rows = basis.shape[1] // lax.axis_size("slab")
    copies = []
    for at, (sector, spans, slab) in enumerate(blocks):
        row = pl.multiple_of((2 * slab + place[0] % 2) * rows, rows)
        column = 0
        for start, count in spans:
            copies.append(
                pltpu.make_async_copy(
                    basis.at[sector, pl.ds(row, rows), pl.ds(first_column(start, place, unit), count * unit)],
                    array.at[at, :, pl.ds(column, count * unit)],
                    sems.at[len(copies)],
                )
            )
            column += count * unit
    return copies


def part_shape(blocks, rows, unit):
    return pltpu.VMEM((len(blocks), rows, sum(count for _, count in blocks[0][1]) * unit), jnp.bfloat16)


def part_sems(blocks):
    return pltpu.SemaphoreType.DMA((sum(len(spans) for _, spans, _ in blocks),))


def half_products(sectors, distances, place, basis, fermion, pieces, ready=lambda sector: None, slots=None):
    flavours, _, _, width = fermion.shape
    for sector in sectors:
        ready(sector)
        right = jnp.concatenate([fermion[flavour, sector] for flavour in range(flavours)], axis=1)
        for slot, distance in enumerate(distances):
            column = slots[slot] if slots else pl.multiple_of((place[0] ^ distance) * width, width)
            block = lax.dot_general(
                basis[sector, :, pl.ds(column, width)],
                right,
                (((0,), (0,)), ((), ())),
                preferred_element_type=jnp.float32,
            ).astype(jnp.bfloat16)
            for flavour in range(flavours):
                pieces[slot][sector, flavour] = block[:, flavour * width : (flavour + 1) * width]


def part_kernel(blocks, unit, distances, place, basis, fermion, sent, *refs):
    *pieces, left, right, sems, half_sems = refs
    width = fermion.shape[3]
    copies = part_copies(blocks, unit, place, basis, sent, sems)
    for copy in copies:
        copy.start()

    @pl.when(place[1] == 0)
    def _():
        held = [
            [
                pltpu.make_async_copy(fermion.at[:, sector], right.at[:, sector], half_sems.at[sector, 0]),
                *(
                    pltpu.make_async_copy(
                        basis.at[sector, :, pl.ds(pl.multiple_of((place[0] ^ distance) * width, width), width)],
                        left.at[sector, :, pl.ds(slot * width, width)],
                        half_sems.at[sector, 1 + slot],
                    )
                    for slot, distance in enumerate(distances)
                ),
            ]
            for sector in range(basis.shape[0])
        ]
        for pair in held:
            for copy in pair:
                copy.start()

        def ready(sector):
            for copy in held[sector]:
                copy.wait()

        slots = [slot * width for slot in range(len(distances))]
        half_products(range(basis.shape[0]), distances, place, left, right, pieces, ready, slots)

    for copy in copies:
        copy.wait()


def basis_part(basis, fermion, blocks, unit, distances):
    flavours, sectors, depth, width = fermion.shape
    shapes = [part_shape(blocks, width, unit)]
    shapes += [pltpu.VMEM((sectors, flavours, width, width), jnp.bfloat16)] * len(distances)
    return kernel_call(
        functools.partial(part_kernel, blocks, unit, distances),
        "part",
        basis.shape[:2],
        [in_hbm(basis), in_hbm(fermion)],
        [ANY, ANY],
        shapes,
        [WHOLE] * len(shapes),
        [
            pltpu.VMEM((sectors, depth, len(distances) * width), jnp.bfloat16),
            pltpu.VMEM((flavours, sectors, depth, width), jnp.bfloat16),
            part_sems(blocks),
            pltpu.SemaphoreType.DMA((sectors, 1 + len(distances))),
        ],
    )


def far_kernel(distances, place, basis, fermion, *refs):
    pieces = refs[len(distances) :]

    @pl.when(place[1] != 0)
    def _():
        half_products(range(basis.shape[0]), distances, place, basis, fermion, pieces)


def far_blocks(basis, fermion, distances, earlier):
    return kernel_call(
        functools.partial(far_kernel, distances),
        "far",
        basis.shape[:2],
        [in_vmem(basis), in_vmem(fermion), *map(in_vmem, earlier)],
        [WHOLE] * (2 + len(earlier)),
        [pltpu.VMEM(piece.shape, piece.dtype) for piece in earlier],
        [WHOLE] * len(distances),
        aliases={2 + at: at for at in range(len(earlier))},
    )


def near_kernel(blocks, unit, distances, place, basis, fermion, _, *refs):
    *pieces, sent, sems = refs
    copies = part_copies(blocks, unit, place, basis, sent, sems)
    for copy in copies:
        copy.start()
    half_products(range(basis.shape[0]), distances, place, basis, fermion, pieces)
    for copy in copies:
        copy.wait()


def near_blocks(basis, fermion, blocks, unit, distances, after):
    flavours, sectors, depth, width = fermion.shape
    return kernel_call(
        functools.partial(near_kernel, blocks, unit, distances),
        "near",
        basis.shape[:2],
        [in_vmem(basis), in_vmem(fermion), in_vmem(after)],
        [WHOLE, WHOLE, WHOLE],
        [pltpu.VMEM((sectors, flavours, width, width), jnp.bfloat16)] * len(distances)
        + [part_shape(blocks, width, unit)],
        [WHOLE] * (len(distances) + 1),
        [part_sems(blocks)],
    )


def cut_kernel(cuts, given, *refs):
    for cut, piece in zip(cuts, refs[-len(cuts) :]):
        piece[...] = given[cut]


def cut_out(array, cuts, after=()):
    shapes = [jax.eval_shape(lambda x, cut=cut: x[cut], array).shape for cut in cuts]
    return kernel_call(
        functools.partial(cut_kernel, cuts),
        "cut",
        None,
        [in_vmem(array), *map(in_vmem, after)],
        [WHOLE] * (1 + len(after)),
        [pltpu.VMEM(shape, array.dtype) for shape in shapes],
        [WHOLE] * len(cuts),
    )


def own_copies(units, unit, place, basis, right, sems, first):
    sectors, depth, _ = basis.shape
    slabs = lax.axis_size("slab")
    rows = depth // slabs
    copies, at = [], 0
    for start, count in units:
        for slab in range(slabs):
            copies.append(
                pltpu.make_async_copy(
                    basis.at[:, pl.ds(slab * rows, rows), pl.ds(first_column(start, place, unit), count * unit)],
                    right.at[pl.ds(0, sectors), slab % 2, slab // 2, :, pl.ds(at, count * unit)],
                    sems.at[first + len(copies)],
                )
            )
        at += count * unit
    return copies


def next_copies(nexts, place, arrays, side, right, sems, first):
    sectors = right.shape[0] // 2
    copies = []
    for array, runs in zip(arrays, nexts):
        index = 0
        for sector, slab, count, column in runs:
            copies.append(
                pltpu.make_async_copy(
                    array.at[pl.ds(index, count)],
                    right.at[
                        sectors + sector, (place[0] + side) % 2, pl.ds(slab, count), :, pl.ds(column, array.shape[2])
                    ],
                    sems.at[first + len(copies)],
                )
            )
            index += count
    return copies


def half_copy(half, distance, place, left, sem):
    slabs = lax.axis_size("slab")
    width = half.shape[3]
    slab = place[0] ^ distance
    column = pl.multiple_of(((slab % 2) * (slabs // 2) + slab // 2) * width, width)
    return pltpu.make_async_copy(half, left.at[:, :, :, pl.ds(column, width)], sem)


def gather_kernel(groups, nexts, unit, distances, cuts, place, basis, *refs):
    halves, refs = refs[: len(distances)], refs[len(distances) :]
    pairs, refs = [refs[2 * i : 2 * i + 2] for i in range(len(nexts))], refs[2 * len(nexts) :]
    left, *rights, sent, sems = refs
    copies = next_copies(nexts, place, [pair[0] for pair in pairs], 0, rights[0], sems, 0)
    copies += next_copies(nexts, place, [pair[1] for pair in pairs], 1, rights[0], sems, len(copies))
    for units, right in zip(groups, rights):
        copies += own_copies(units, unit, place, basis, right, sems, len(copies))
    for half, distance in zip(halves, distances):
        copies.append(half_copy(half, distance, place, left, sems.at[len(copies)]))
    for at, cut in enumerate(cuts):
        copies.append(pltpu.make_async_copy(pairs[-1][0].at[cut], sent.at[at], sems.at[len(copies)]))
    run(copies)


def gather(basis, groups, nexts, unit, pairs, halves, distances, cuts):
    sectors, depth, _ = basis.shape
    flavours, width = halves[0].shape[1:3]
    given = [in_vmem(array) for array in (basis, *halves, *(array for pair in pairs for array in pair))]
    copies = sum(map(len, groups)) * (depth // width) + 2 * sum(len(holds) for holds in nexts)
    shapes = [pltpu.VMEM((sectors, flavours, width, depth), jnp.bfloat16)]
    for units in groups:
        columns = sum(count for _, count in units) * unit
        shapes.append(pltpu.VMEM((2 * sectors, 2, depth // width // 2, width, columns), jnp.bfloat16))
    shapes.append(pltpu.VMEM((len(cuts), width, unit), jnp.bfloat16))
    return kernel_call(
        functools.partial(gather_kernel, groups, nexts, unit, distances, cuts),
        "gather",
        basis.shape[:2],
        given,
        [WHOLE] * len(given),
        shapes,
        [WHOLE] * len(shapes),
        [pltpu.SemaphoreType.DMA((copies + len(halves) + len(cuts),))],
    )


def product(place, partner, sector, flavour, left, right):
    index = (partner[...][sector, flavour] - place[1] + place[2]) % place[2]
    rows = right[index].reshape(left.shape[3], right.shape[4])
    return jnp.dot(left[sector, flavour], rows, preferred_element_type=jnp.float32).astype(jnp.bfloat16)


def write_out(units, unit, place, sector, flavour, stage, out, sems):
    copies, at = [], 0
    for number, (start, count) in enumerate(units):
        copies.append(
            pltpu.make_async_copy(
                stage.at[flavour, sector, :, pl.ds(at, count * unit)],
                out.at[flavour, sector, :, pl.ds(first_column(start, place, unit), count * unit)],
                sems.at[sector * stage.shape[0] + flavour, number],
            )
        )
        copies[-1].start()
        at += count * unit
    return copies


def early_kernel(units, unit, distance, place, partner, half, right, _, left, out, stage, sem, out_sems):
    run([half_copy(half, distance, place, left, sem)])
    sectors, flavours = left.shape[:2]
    copies = []
    for sector in range(sectors):
        for flavour in range(flavours):
            stage[flavour, sector] = product(place, partner, sector, flavour, left, right)
            copies += write_out(units, unit, place, sector, flavour, stage, out, out_sems)
    for copy in copies:
        copy.wait()


def early_products(partner, half, distance, units, unit, left, right):
    sectors, flavours, width, depth = left.shape
    return kernel_call(
        functools.partial(early_kernel, units, unit, distance),
        "early",
        (sectors, depth),
        [partner, in_vmem(half), in_vmem(right), in_vmem(left)],
        [WHOLE] * 4,
        [
            pltpu.VMEM(left.shape, left.dtype),
            pltpu.HBM((flavours, sectors, width, depth), jnp.bfloat16),
        ],
        [WHOLE, ANY],
        [
            pltpu.VMEM((flavours, sectors, width, right.shape[4]), jnp.bfloat16),
            pltpu.SemaphoreType.DMA,
            pltpu.SemaphoreType.DMA((sectors * flavours, len(units))),
        ],
        {3: 0},
    )


def partial(place, partner, sector, flavour, side, left, right):
    index = (partner[...][sector, flavour] - place[1] + place[2]) % place[2]
    core = (place[0] + side) % 2
    half = left.shape[3] // 2
    rows = right[index, core].reshape(half, right.shape[4])
    columns = pl.ds(pl.multiple_of(core * half, half), half)
    return jnp.dot(left[sector, flavour, :, columns], rows, preferred_element_type=jnp.float32)


def own_rows_kernel(groups, place, partner, left, *refs):
    arrays = []
    for nexts in groups:
        arrays.append(refs[: len(nexts)])
        refs = refs[len(nexts) :]
    refs = refs[len(groups) :]
    totals, rights, sems = refs[: len(groups)], refs[len(groups) : 2 * len(groups)], refs[2 * len(groups) :]
    copies = [
        next_copies(nexts, place, here, 0, right, sem, 0)
        for nexts, here, right, sem in zip(groups, arrays, rights, sems)
    ]
    for group in copies:
        for copy in group:
            copy.start()
    sectors, flavours = left.shape[:2]
    for group, total, right in zip(copies, totals, rights):
        for copy in group:
            copy.wait()
        for sector in range(sectors):
            for flavour in range(flavours):
                total[flavour, sector] = partial(place, partner, sector, flavour, 0, left, right)


def own_rows(partner, groups, arrays, left, rights):
    sectors, flavours, width, depth = left.shape
    given = [in_vmem(array) for array in (left, *(array for group in arrays for array in group), *rights)]
    first = 1 + len(given) - len(rights)
    return kernel_call(
        functools.partial(own_rows_kernel, groups),
        "own_rows",
        (sectors, depth),
        [partner, *given],
        [WHOLE] * (1 + len(given)),
        [pltpu.VMEM((flavours, sectors, width, right.shape[4]), jnp.float32) for right in rights]
        + [pltpu.VMEM(right.shape, right.dtype) for right in rights],
        [WHOLE] * (2 * len(rights)),
        [pltpu.SemaphoreType.DMA((sum(map(len, nexts)),)) for nexts in groups],
        {first + at: len(rights) + at for at in range(len(rights))},
    )


def late_kernel(units, nexts, unit, place, partner, left, total, *refs):
    arrays, (_, _, out, right, stage, sems, out_sems) = refs[: len(nexts)], refs[len(nexts) :]
    sectors, flavours = left.shape[:2]
    run(next_copies(nexts, place, arrays, 1, right, sems, 0))
    copies = []
    for sector in range(sectors):
        for flavour in range(flavours):
            rest = partial(place, partner, sector, flavour, 1, left, right)
            stage[flavour, sector] = (total[flavour, sector] + rest).astype(jnp.bfloat16)
            copies += write_out(units, unit, place, sector, flavour, stage, out, out_sems)
    for copy in copies:
        copy.wait()


def late_products(partner, units, nexts, unit, arrays, left, total, right, out):
    sectors, flavours, width, depth = left.shape
    given = [in_vmem(array) for array in (left, total, *arrays, right)]
    return kernel_call(
        functools.partial(late_kernel, units, nexts, unit),
        "late",
        (sectors, depth),
        [partner, *given, out],
        [WHOLE] * (1 + len(given)) + [ANY],
        [pltpu.HBM(out.shape, out.dtype), pltpu.VMEM(right.shape, right.dtype)],
        [ANY, WHOLE],
        [
            pltpu.VMEM((flavours, sectors, width, right.shape[4]), jnp.bfloat16),
            pltpu.SemaphoreType.DMA((sum(map(len, nexts)),)),
            pltpu.SemaphoreType.DMA((sectors * flavours, len(units))),
        ],
        {len(given): 1, 1 + len(given): 0},
    )[0]


def local(basis, fermion, partner):
    sectors, depth, _ = basis.shape
    unit = depth // 8
    partner = partner.T
    distances = tuple(reversed(range(lax.axis_size("slab"))))
    slabs = range(lax.axis_size("slab") // 2)
    held = [(sector, slab) for sector in range(sectors) for slab in slabs]
    alone = len(held) // 4
    count = 3
    units = ((0, count), (OWN, 1)), ((count, 6 - count), (OTHER, 1))
    first_blocks = [(sector, units[0], slab) for sector, slab in held]
    last_blocks = [(sector, ((start, 1),), slab) for start in range(count, 6) for sector, slab in held]
    last_blocks += [(sector, ((OTHER, 1),), slab) for sector, slab in held[:alone]]
    first_part, *far = basis_part(basis, fermion, first_blocks, unit, distances[:2])
    first = previous(first_part)
    far3, far2 = far_blocks(basis, fermion, distances[:2], far)
    got3, got2 = swapped(far3, distances[0]), swapped(far2, distances[1])
    mine, near, last_part = near_blocks(basis, fermion, last_blocks, unit, distances[2:], far2)
    beside, last = swapped(mine, distances[2]), previous(last_part)

    def runs(column, blocks):
        found = []
        for sector, slab in blocks:
            if found and found[-1][0] == sector:
                found[-1][2] += 1
            else:
                found.append([sector, slab, 1, column])
        return found

    groups = ((0, 2), (2, 4))
    every = slice(None)
    pieces = cut_out(first, [(every, every, slice(begin * unit, end * unit)) for begin, end in groups], (beside, got2))
    pairs = [(piece, swapped(piece, 1)) for piece in pieces]
    nexts = [runs(begin * unit, held) for begin, _ in groups]
    cuts = [(at, every, pl.ds((groups[-1][1] - groups[-1][0] - 1) * unit, unit)) for at in range(alone, len(held))]
    left, early_right, late_right, sent = gather(
        basis, units, nexts, unit, pairs, [got2, beside, near], distances[1:], cuts
    )
    other = swapped(sent, distances[1])
    left, out = early_products(partner, got3, distances[0], units[0], unit, left, early_right)
    last, other, out = lax.optimization_barrier((last, other, out))
    last_other, other_other = swapped(last, 1), swapped(other, 1)
    nexts = [[], runs((6 - count) * unit, held[alone:])]
    for at in range(6 - count):
        nexts[0] += runs(at * unit, held)
    nexts[0] += runs((6 - count) * unit, held[:alone])
    total, late_right = own_rows(partner, [nexts], [[last, other]], left, [late_right])
    return late_products(partner, units[1], nexts, unit, [last_other, other_other], left, total, late_right, out)


def solution(mesh):
    placed = (P("sec", None, None), P(None, "sec", None, "slab"), P(None, "sec"))
    return jax.shard_map(
        local, mesh=mesh, in_specs=placed, out_specs=P(None, "sec", "slab", None), check_vma=False
    )
```

```python
import functools

import jax
import jax.numpy as jnp
from jax import lax
from jax.experimental import pallas as pl
from jax.experimental.pallas import tpu as pltpu
from jax.sharding import PartitionSpec as P

ANY = pl.BlockSpec(memory_space=pl.ANY)
WHOLE = pl.BlockSpec(memory_space=pltpu.VMEM)
OWN, OTHER = -1, -2
KERNEL_BYTES = 16 * 1024 * 1024
BRIEF = pl.CostEstimate(flops=0, bytes_accessed=0, transcendentals=0)


def in_hbm(array):
    return pltpu.with_memory_space_constraint(array, pltpu.HBM)


def in_vmem(array):
    return pltpu.with_memory_space_constraint(array, pltpu.VMEM)


def located(sectors, depth):
    first = lax.axis_index("sec") * sectors
    return lax.axis_index("slab"), first, lax.axis_size("sec") * sectors, depth - depth // 8 * 2


def kernel_call(body, name, shape, given, specs, shapes, out_specs, scratch=(), aliases={}, cost=BRIEF):
    def kernel(*refs):
        body(*(() if shape is None else (located(*shape),)), *refs)

    return pl.pallas_call(
        kernel,
        out_shape=shapes,
        in_specs=specs,
        out_specs=out_specs,
        scratch_shapes=list(scratch),
        input_output_aliases=aliases,
        compiler_params=pltpu.CompilerParams(vmem_limit_bytes=KERNEL_BYTES),
        cost_estimate=cost,
        name=name,
    )(*given)


def first_column(unit, place, width):
    if unit == OWN:
        return pl.multiple_of(place[3] + (place[0] // 2) * width, width)
    if unit == OTHER:
        return pl.multiple_of(place[3] + (1 - place[0] // 2) * width, width)
    return unit * width


def run(copies):
    for copy in copies:
        copy.start()
    for copy in copies:
        copy.wait()


def previous(block):
    count = lax.axis_size("sec")
    return lax.ppermute(block, "sec", [((i + 1) % count, i) for i in range(count)])


def swapped(block, distance):
    return lax.ppermute(block, "slab", [(i, i ^ distance) for i in range(lax.axis_size("slab"))])


def part_copies(blocks, unit, place, basis, array, sems):
    rows = basis.shape[1] // lax.axis_size("slab")
    copies = []
    for at, (sector, spans, slab) in enumerate(blocks):
        row = pl.multiple_of((2 * slab + place[0] % 2) * rows, rows)
        column = 0
        for start, count in spans:
            copies.append(
                pltpu.make_async_copy(
                    basis.at[sector, pl.ds(row, rows), pl.ds(first_column(start, place, unit), count * unit)],
                    array.at[at, :, pl.ds(column, count * unit)],
                    sems.at[len(copies)],
                )
            )
            column += count * unit
    return copies


def part_shape(blocks, rows, unit):
    return pltpu.VMEM((len(blocks), rows, sum(count for _, count in blocks[0][1]) * unit), jnp.bfloat16)


def part_sems(blocks):
    return pltpu.SemaphoreType.DMA((sum(len(spans) for _, spans, _ in blocks),))


def half_products(sectors, distances, place, basis, fermion, pieces, ready=lambda sector: None, slots=None):
    flavours, _, _, width = fermion.shape
    for sector in sectors:
        ready(sector)
        right = jnp.concatenate([fermion[flavour, sector] for flavour in range(flavours)], axis=1)
        for slot, distance in enumerate(distances):
            column = slots[slot] if slots else pl.multiple_of((place[0] ^ distance) * width, width)
            block = lax.dot_general(
                basis[sector, :, pl.ds(column, width)],
                right,
                (((0,), (0,)), ((), ())),
                preferred_element_type=jnp.float32,
            ).astype(jnp.bfloat16)
            for flavour in range(flavours):
                pieces[slot][sector, flavour] = block[:, flavour * width : (flavour + 1) * width]


def part_kernel(blocks, unit, distances, place, basis, fermion, sent, *refs):
    *pieces, left, right, sems, half_sems = refs
    width = fermion.shape[3]
    copies = part_copies(blocks, unit, place, basis, sent, sems)
    for copy in copies:
        copy.start()

    @pl.when(place[1] == 0)
    def _():
        held = [
            [
                pltpu.make_async_copy(fermion.at[:, sector], right.at[:, sector], half_sems.at[sector, 0]),
                *(
                    pltpu.make_async_copy(
                        basis.at[sector, :, pl.ds(pl.multiple_of((place[0] ^ distance) * width, width), width)],
                        left.at[sector, :, pl.ds(slot * width, width)],
                        half_sems.at[sector, 1 + slot],
                    )
                    for slot, distance in enumerate(distances)
                ),
            ]
            for sector in range(basis.shape[0])
        ]
        for pair in held:
            for copy in pair:
                copy.start()

        def ready(sector):
            for copy in held[sector]:
                copy.wait()

        slots = [slot * width for slot in range(len(distances))]
        half_products(range(basis.shape[0]), distances, place, left, right, pieces, ready, slots)

    for copy in copies:
        copy.wait()


def basis_part(basis, fermion, blocks, unit, distances):
    flavours, sectors, depth, width = fermion.shape
    shapes = [part_shape(blocks, width, unit)]
    shapes += [pltpu.VMEM((sectors, flavours, width, width), jnp.bfloat16)] * len(distances)
    return kernel_call(
        functools.partial(part_kernel, blocks, unit, distances),
        "part",
        basis.shape[:2],
        [in_hbm(basis), in_hbm(fermion)],
        [ANY, ANY],
        shapes,
        [WHOLE] * len(shapes),
        [
            pltpu.VMEM((sectors, depth, len(distances) * width), jnp.bfloat16),
            pltpu.VMEM((flavours, sectors, depth, width), jnp.bfloat16),
            part_sems(blocks),
            pltpu.SemaphoreType.DMA((sectors, 1 + len(distances))),
        ],
    )


def far_kernel(distances, place, basis, fermion, *refs):
    pieces = refs[len(distances) :]

    @pl.when(place[1] != 0)
    def _():
        half_products(range(basis.shape[0]), distances, place, basis, fermion, pieces)


def far_blocks(basis, fermion, distances, earlier):
    return kernel_call(
        functools.partial(far_kernel, distances),
        "far",
        basis.shape[:2],
        [in_vmem(basis), in_vmem(fermion), *map(in_vmem, earlier)],
        [WHOLE] * (2 + len(earlier)),
        [pltpu.VMEM(piece.shape, piece.dtype) for piece in earlier],
        [WHOLE] * len(distances),
        aliases={2 + at: at for at in range(len(earlier))},
    )


def near_kernel(blocks, unit, distances, place, basis, fermion, _, *refs):
    *pieces, sent, sems = refs
    copies = part_copies(blocks, unit, place, basis, sent, sems)
    for copy in copies:
        copy.start()
    half_products(range(basis.shape[0]), distances, place, basis, fermion, pieces)
    for copy in copies:
        copy.wait()


def near_blocks(basis, fermion, blocks, unit, distances, after):
    flavours, sectors, depth, width = fermion.shape
    return kernel_call(
        functools.partial(near_kernel, blocks, unit, distances),
        "near",
        basis.shape[:2],
        [in_vmem(basis), in_vmem(fermion), in_vmem(after)],
        [WHOLE, WHOLE, WHOLE],
        [pltpu.VMEM((sectors, flavours, width, width), jnp.bfloat16)] * len(distances)
        + [part_shape(blocks, width, unit)],
        [WHOLE] * (len(distances) + 1),
        [part_sems(blocks)],
    )


def cut_kernel(cuts, given, *refs):
    for cut, piece in zip(cuts, refs[-len(cuts) :]):
        piece[...] = given[cut]


def cut_out(array, cuts, after=()):
    shapes = [jax.eval_shape(lambda x, cut=cut: x[cut], array).shape for cut in cuts]
    return kernel_call(
        functools.partial(cut_kernel, cuts),
        "cut",
        None,
        [in_vmem(array), *map(in_vmem, after)],
        [WHOLE] * (1 + len(after)),
        [pltpu.VMEM(shape, array.dtype) for shape in shapes],
        [WHOLE] * len(cuts),
    )


def own_copies(units, unit, place, basis, right, sems, first):
    sectors, depth, _ = basis.shape
    slabs = lax.axis_size("slab")
    rows = depth // slabs
    copies, at = [], 0
    for start, count in units:
        for slab in range(slabs):
            copies.append(
                pltpu.make_async_copy(
                    basis.at[:, pl.ds(slab * rows, rows), pl.ds(first_column(start, place, unit), count * unit)],
                    right.at[pl.ds(0, sectors), slab % 2, slab // 2, :, pl.ds(at, count * unit)],
                    sems.at[first + len(copies)],
                )
            )
        at += count * unit
    return copies


def next_copies(nexts, place, arrays, side, right, sems, first):
    sectors = right.shape[0] // 2
    copies = []
    for array, runs in zip(arrays, nexts):
        index = 0
        for sector, slab, count, column in runs:
            copies.append(
                pltpu.make_async_copy(
                    array.at[pl.ds(index, count)],
                    right.at[
                        sectors + sector, (place[0] + side) % 2, pl.ds(slab, count), :, pl.ds(column, array.shape[2])
                    ],
                    sems.at[first + len(copies)],
                )
            )
            index += count
    return copies


def half_copy(half, distance, place, left, sem):
    slabs = lax.axis_size("slab")
    width = half.shape[3]
    slab = place[0] ^ distance
    column = pl.multiple_of(((slab % 2) * (slabs // 2) + slab // 2) * width, width)
    return pltpu.make_async_copy(half, left.at[:, :, :, pl.ds(column, width)], sem)


def gather_kernel(groups, nexts, unit, distances, cuts, place, basis, *refs):
    halves, refs = refs[: len(distances)], refs[len(distances) :]
    pairs, refs = [refs[2 * i : 2 * i + 2] for i in range(len(nexts))], refs[2 * len(nexts) :]
    left, *rights, sent, sems = refs
    copies = next_copies(nexts, place, [pair[0] for pair in pairs], 0, rights[0], sems, 0)
    copies += next_copies(nexts, place, [pair[1] for pair in pairs], 1, rights[0], sems, len(copies))
    for units, right in zip(groups, rights):
        copies += own_copies(units, unit, place, basis, right, sems, len(copies))
    for half, distance in zip(halves, distances):
        copies.append(half_copy(half, distance, place, left, sems.at[len(copies)]))
    for at, cut in enumerate(cuts):
        copies.append(pltpu.make_async_copy(pairs[-1][0].at[cut], sent.at[at], sems.at[len(copies)]))
    run(copies)


def gather(basis, groups, nexts, unit, pairs, halves, distances, cuts):
    sectors, depth, _ = basis.shape
    flavours, width = halves[0].shape[1:3]
    given = [in_vmem(array) for array in (basis, *halves, *(array for pair in pairs for array in pair))]
    copies = sum(map(len, groups)) * (depth // width) + 2 * sum(len(holds) for holds in nexts)
    shapes = [pltpu.VMEM((sectors, flavours, width, depth), jnp.bfloat16)]
    for units in groups:
        columns = sum(count for _, count in units) * unit
        shapes.append(pltpu.VMEM((2 * sectors, 2, depth // width // 2, width, columns), jnp.bfloat16))
    shapes.append(pltpu.VMEM((len(cuts), width, unit), jnp.bfloat16))
    return kernel_call(
        functools.partial(gather_kernel, groups, nexts, unit, distances, cuts),
        "gather",
        basis.shape[:2],
        given,
        [WHOLE] * len(given),
        shapes,
        [WHOLE] * len(shapes),
        [pltpu.SemaphoreType.DMA((copies + len(halves) + len(cuts),))],
    )


def product(place, partner, sector, flavour, left, right):
    index = (partner[...][sector, flavour] - place[1] + place[2]) % place[2]
    rows = right[index].reshape(left.shape[3], right.shape[4])
    return jnp.dot(left[sector, flavour], rows, preferred_element_type=jnp.float32).astype(jnp.bfloat16)


def early_kernel(distance, place, partner, half, right, _, left, stage, sem):
    run([half_copy(half, distance, place, left, sem)])
    sectors, flavours = left.shape[:2]
    for sector in range(sectors):
        for flavour in range(flavours):
            stage[flavour, sector] = product(place, partner, sector, flavour, left, right)


def early_products(partner, half, distance, left, right):
    sectors, flavours, width, _ = left.shape
    return kernel_call(
        functools.partial(early_kernel, distance),
        "early",
        (left.shape[0], left.shape[3]),
        [partner, in_vmem(half), in_vmem(right), in_vmem(left)],
        [WHOLE] + [WHOLE] * 3,
        [
            pltpu.VMEM(left.shape, left.dtype),
            pltpu.VMEM((flavours, sectors, width, right.shape[4]), jnp.bfloat16),
        ],
        [WHOLE] * 2,
        [pltpu.SemaphoreType.DMA],
        {3: 0},
    )


def partial(place, partner, sector, flavour, side, left, right):
    index = (partner[...][sector, flavour] - place[1] + place[2]) % place[2]
    core = (place[0] + side) % 2
    half = left.shape[3] // 2
    rows = right[index, core].reshape(half, right.shape[4])
    columns = pl.ds(pl.multiple_of(core * half, half), half)
    return jnp.dot(left[sector, flavour, :, columns], rows, preferred_element_type=jnp.float32)


def own_rows_kernel(groups, place, partner, left, *refs):
    arrays = []
    for nexts in groups:
        arrays.append(refs[: len(nexts)])
        refs = refs[len(nexts) :]
    refs = refs[len(groups) :]
    totals, rights, sems = refs[: len(groups)], refs[len(groups) : 2 * len(groups)], refs[2 * len(groups) :]
    copies = [
        next_copies(nexts, place, here, 0, right, sem, 0)
        for nexts, here, right, sem in zip(groups, arrays, rights, sems)
    ]
    for group in copies:
        for copy in group:
            copy.start()
    sectors, flavours = left.shape[:2]
    for group, total, right in zip(copies, totals, rights):
        for copy in group:
            copy.wait()
        for sector in range(sectors):
            for flavour in range(flavours):
                total[flavour, sector] = partial(place, partner, sector, flavour, 0, left, right)


def own_rows(partner, groups, arrays, left, rights):
    sectors, flavours, width, depth = left.shape
    given = [in_vmem(array) for array in (left, *(array for group in arrays for array in group), *rights)]
    first = 1 + len(given) - len(rights)
    return kernel_call(
        functools.partial(own_rows_kernel, groups),
        "own_rows",
        (sectors, depth),
        [partner, *given],
        [WHOLE] * (1 + len(given)),
        [pltpu.VMEM((flavours, sectors, width, right.shape[4]), jnp.float32) for right in rights]
        + [pltpu.VMEM(right.shape, right.dtype) for right in rights],
        [WHOLE] * (2 * len(rights)),
        [pltpu.SemaphoreType.DMA((sum(map(len, nexts)),)) for nexts in groups],
        {first + at: len(rights) + at for at in range(len(rights))},
    )


def late_kernel(earlier_units, units, nexts, unit, place, partner, left, total, *refs):
    earlier, refs = refs[: len(earlier_units)], refs[len(earlier_units) :]
    arrays, (_, out, right, stage, sems, early_sems, out_sems) = refs[: len(nexts)], refs[len(nexts) :]
    sectors, flavours = left.shape[:2]
    next_here = next_copies(nexts, place, arrays, 1, right, sems, 0)
    for copy in next_here:
        copy.start()
    out_copies = []
    for result, spans in zip(earlier, earlier_units):
        at = 0
        for start, count in spans:
            out_copies.append(
                pltpu.make_async_copy(
                    result.at[:, :, :, pl.ds(at, count * unit)],
                    out.at[:, :, :, pl.ds(first_column(start, place, unit), count * unit)],
                    early_sems.at[len(out_copies)],
                )
            )
            out_copies[-1].start()
            at += count * unit
    for copy in next_here:
        copy.wait()
    for sector in range(sectors):
        for flavour in range(flavours):
            rest = partial(place, partner, sector, flavour, 1, left, right)
            stage[flavour, sector] = (total[flavour, sector] + rest).astype(jnp.bfloat16)
            at = 0
            for number, (start, count) in enumerate(units):
                copy = pltpu.make_async_copy(
                    stage.at[flavour, sector, :, pl.ds(at, count * unit)],
                    out.at[flavour, sector, :, pl.ds(first_column(start, place, unit), count * unit)],
                    out_sems.at[sector * flavours + flavour, number],
                )
                copy.start()
                out_copies.append(copy)
                at += count * unit
    for copy in out_copies:
        copy.wait()


def late_products(partner, groups, nexts, unit, arrays, left, total, earlier, right):
    sectors, flavours, width, depth = left.shape
    given = [in_vmem(array) for array in (left, total, *earlier, *arrays, right)]
    return kernel_call(
        functools.partial(late_kernel, groups[:-1], groups[-1], nexts, unit),
        "late",
        (sectors, depth),
        [partner, *given],
        [WHOLE] * (1 + len(given)),
        [
            pltpu.HBM((flavours, sectors, width, depth), jnp.bfloat16),
            pltpu.VMEM(right.shape, right.dtype),
        ],
        [ANY, WHOLE],
        [
            pltpu.VMEM((flavours, sectors, width, right.shape[4]), jnp.bfloat16),
            pltpu.SemaphoreType.DMA((sum(map(len, nexts)),)),
            pltpu.SemaphoreType.DMA((sum(map(len, groups[:-1])),)),
            pltpu.SemaphoreType.DMA((sectors * flavours, len(groups[-1]))),
        ],
        {len(given): 1},
    )[0]


def local(basis, fermion, partner):
    sectors, depth, _ = basis.shape
    unit = depth // 8
    partner = partner.T
    distances = tuple(reversed(range(lax.axis_size("slab"))))
    slabs = range(lax.axis_size("slab") // 2)
    held = [(sector, slab) for sector in range(sectors) for slab in slabs]
    alone = len(held) // 4
    count = 3
    units = ((0, count), (OWN, 1)), ((count, 6 - count), (OTHER, 1))
    first_blocks = [(sector, units[0], slab) for sector, slab in held]
    last_blocks = [(sector, ((start, 1),), slab) for start in range(count, 6) for sector, slab in held]
    last_blocks += [(sector, ((OTHER, 1),), slab) for sector, slab in held[:alone]]
    first_part, *far = basis_part(basis, fermion, first_blocks, unit, distances[1:2])
    first = previous(first_part)
    far2 = far_blocks(basis, fermion, distances[1:2], far)[0]
    rest = distances[:1] + distances[2:]
    far3, mine, near, last_part = near_blocks(basis, fermion, last_blocks, unit, rest, far2)
    got3, got2 = swapped(far3, distances[0]), swapped(far2, distances[1])
    beside, last = swapped(mine, distances[2]), previous(last_part)

    def runs(column, blocks):
        found = []
        for sector, slab in blocks:
            if found and found[-1][0] == sector:
                found[-1][2] += 1
            else:
                found.append([sector, slab, 1, column])
        return found

    groups = ((0, 2), (2, 4))
    every = slice(None)
    pieces = cut_out(first, [(every, every, slice(begin * unit, end * unit)) for begin, end in groups], (beside, got2))
    pairs = [(piece, swapped(piece, 1)) for piece in pieces]
    nexts = [runs(begin * unit, held) for begin, _ in groups]
    cuts = [(at, every, pl.ds((groups[-1][1] - groups[-1][0] - 1) * unit, unit)) for at in range(alone, len(held))]
    left, early_right, late_right, sent = gather(
        basis, units, nexts, unit, pairs, [got2, beside, near], distances[1:], cuts
    )
    other = swapped(sent, distances[1])
    left, early = early_products(partner, got3, distances[0], left, early_right)
    last, other, early = lax.optimization_barrier((last, other, early))
    last_other, other_other = swapped(last, 1), swapped(other, 1)
    nexts = [[], runs((6 - count) * unit, held[alone:])]
    for at in range(6 - count):
        nexts[0] += runs(at * unit, held)
    nexts[0] += runs((6 - count) * unit, held[:alone])
    total, late_right = own_rows(partner, [nexts], [[last, other]], left, [late_right])
    return late_products(
        partner, units, nexts, unit, [last_other, other_other], left, total, [early], late_right
    )


def solution(mesh):
    placed = (P("sec", None, None), P(None, "sec", None, "slab"), P(None, "sec"))
    return jax.shard_map(
        local, mesh=mesh, in_specs=placed, out_specs=P(None, "sec", "slab", None), check_vma=False
    )
```

```python
import functools

import jax
import jax.numpy as jnp
from jax import lax
from jax.experimental import pallas as pl
from jax.experimental.pallas import tpu as pltpu
from jax.sharding import PartitionSpec as P

ANY = pl.BlockSpec(memory_space=pl.ANY)
WHOLE = pl.BlockSpec(memory_space=pltpu.VMEM)
OWN, OTHER = -1, -2
KERNEL_BYTES = 16 * 1024 * 1024
BRIEF = pl.CostEstimate(flops=0, bytes_accessed=0, transcendentals=0)


def in_hbm(array):
    return pltpu.with_memory_space_constraint(array, pltpu.HBM)


def in_vmem(array):
    return pltpu.with_memory_space_constraint(array, pltpu.VMEM)


def located(sectors, depth):
    first = lax.axis_index("sec") * sectors
    return lax.axis_index("slab"), first, lax.axis_size("sec") * sectors, depth - depth // 8 * 2


def kernel_call(body, name, shape, given, specs, shapes, out_specs, scratch=(), aliases={}, cost=BRIEF):
    def kernel(*refs):
        body(*(() if shape is None else (located(*shape),)), *refs)

    return pl.pallas_call(
        kernel,
        out_shape=shapes,
        in_specs=specs,
        out_specs=out_specs,
        scratch_shapes=list(scratch),
        input_output_aliases=aliases,
        compiler_params=pltpu.CompilerParams(vmem_limit_bytes=KERNEL_BYTES),
        cost_estimate=cost,
        name=name,
    )(*given)


def first_column(unit, place, width):
    if unit == OWN:
        return pl.multiple_of(place[3] + (place[0] // 2) * width, width)
    if unit == OTHER:
        return pl.multiple_of(place[3] + (1 - place[0] // 2) * width, width)
    return unit * width


def run(copies):
    for copy in copies:
        copy.start()
    for copy in copies:
        copy.wait()


def previous(block):
    count = lax.axis_size("sec")
    return lax.ppermute(block, "sec", [((i + 1) % count, i) for i in range(count)])


def swapped(block, distance):
    return lax.ppermute(block, "slab", [(i, i ^ distance) for i in range(lax.axis_size("slab"))])


def part_copies(blocks, unit, place, basis, array, sems):
    rows = basis.shape[1] // lax.axis_size("slab")
    copies = []
    for at, (sector, spans, slab) in enumerate(blocks):
        row = pl.multiple_of((2 * slab + place[0] % 2) * rows, rows)
        column = 0
        for start, count in spans:
            copies.append(
                pltpu.make_async_copy(
                    basis.at[sector, pl.ds(row, rows), pl.ds(first_column(start, place, unit), count * unit)],
                    array.at[at, :, pl.ds(column, count * unit)],
                    sems.at[len(copies)],
                )
            )
            column += count * unit
    return copies


def part_shape(blocks, rows, unit):
    return pltpu.VMEM((len(blocks), rows, sum(count for _, count in blocks[0][1]) * unit), jnp.bfloat16)


def part_sems(blocks):
    return pltpu.SemaphoreType.DMA((sum(len(spans) for _, spans, _ in blocks),))


def half_products(sectors, distances, place, basis, fermion, pieces, ready=lambda sector: None, slots=None):
    flavours, _, _, width = fermion.shape
    for sector in sectors:
        ready(sector)
        right = jnp.concatenate([fermion[flavour, sector] for flavour in range(flavours)], axis=1)
        for slot, distance in enumerate(distances):
            column = slots[slot] if slots else pl.multiple_of((place[0] ^ distance) * width, width)
            block = lax.dot_general(
                basis[sector, :, pl.ds(column, width)],
                right,
                (((0,), (0,)), ((), ())),
                preferred_element_type=jnp.float32,
            ).astype(jnp.bfloat16)
            for flavour in range(flavours):
                pieces[slot][sector, flavour] = block[:, flavour * width : (flavour + 1) * width]


def part_kernel(blocks, unit, distances, place, basis, fermion, sent, *refs):
    *pieces, left, right, sems, half_sems = refs
    width = fermion.shape[3]
    copies = part_copies(blocks, unit, place, basis, sent, sems)
    for copy in copies:
        copy.start()

    @pl.when(place[1] == 0)
    def _():
        held = [
            [
                pltpu.make_async_copy(fermion.at[:, sector], right.at[:, sector], half_sems.at[sector, 0]),
                *(
                    pltpu.make_async_copy(
                        basis.at[sector, :, pl.ds(pl.multiple_of((place[0] ^ distance) * width, width), width)],
                        left.at[sector, :, pl.ds(slot * width, width)],
                        half_sems.at[sector, 1 + slot],
                    )
                    for slot, distance in enumerate(distances)
                ),
            ]
            for sector in range(basis.shape[0])
        ]
        for pair in held:
            for copy in pair:
                copy.start()

        def ready(sector):
            for copy in held[sector]:
                copy.wait()

        slots = [slot * width for slot in range(len(distances))]
        half_products(range(basis.shape[0]), distances, place, left, right, pieces, ready, slots)

    for copy in copies:
        copy.wait()


def basis_part(basis, fermion, blocks, unit, distances):
    flavours, sectors, depth, width = fermion.shape
    shapes = [part_shape(blocks, width, unit)]
    shapes += [pltpu.VMEM((sectors, flavours, width, width), jnp.bfloat16)] * len(distances)
    return kernel_call(
        functools.partial(part_kernel, blocks, unit, distances),
        "part",
        basis.shape[:2],
        [in_hbm(basis), in_hbm(fermion)],
        [ANY, ANY],
        shapes,
        [WHOLE] * len(shapes),
        [
            pltpu.VMEM((sectors, depth, len(distances) * width), jnp.bfloat16),
            pltpu.VMEM((flavours, sectors, depth, width), jnp.bfloat16),
            part_sems(blocks),
            pltpu.SemaphoreType.DMA((sectors, 1 + len(distances))),
        ],
    )


def far_kernel(distances, place, basis, fermion, *refs):
    pieces = refs[len(distances) :]

    @pl.when(place[1] != 0)
    def _():
        half_products(range(basis.shape[0]), distances, place, basis, fermion, pieces)


def far_blocks(basis, fermion, distances, earlier):
    return kernel_call(
        functools.partial(far_kernel, distances),
        "far",
        basis.shape[:2],
        [in_vmem(basis), in_vmem(fermion), *map(in_vmem, earlier)],
        [WHOLE] * (2 + len(earlier)),
        [pltpu.VMEM(piece.shape, piece.dtype) for piece in earlier],
        [WHOLE] * len(distances),
        aliases={2 + at: at for at in range(len(earlier))},
    )


def near_kernel(blocks, unit, distances, place, basis, fermion, _, *refs):
    *pieces, sent, sems = refs
    copies = part_copies(blocks, unit, place, basis, sent, sems)
    for copy in copies:
        copy.start()
    half_products(range(basis.shape[0]), distances, place, basis, fermion, pieces)
    for copy in copies:
        copy.wait()


def near_blocks(basis, fermion, blocks, unit, distances, after):
    flavours, sectors, depth, width = fermion.shape
    return kernel_call(
        functools.partial(near_kernel, blocks, unit, distances),
        "near",
        basis.shape[:2],
        [in_vmem(basis), in_vmem(fermion), in_vmem(after)],
        [WHOLE, WHOLE, WHOLE],
        [pltpu.VMEM((sectors, flavours, width, width), jnp.bfloat16)] * len(distances)
        + [part_shape(blocks, width, unit)],
        [WHOLE] * (len(distances) + 1),
        [part_sems(blocks)],
    )


def cut_kernel(cuts, given, *refs):
    for cut, piece in zip(cuts, refs[-len(cuts) :]):
        piece[...] = given[cut]


def cut_out(array, cuts, after=()):
    shapes = [jax.eval_shape(lambda x, cut=cut: x[cut], array).shape for cut in cuts]
    return kernel_call(
        functools.partial(cut_kernel, cuts),
        "cut",
        None,
        [in_vmem(array), *map(in_vmem, after)],
        [WHOLE] * (1 + len(after)),
        [pltpu.VMEM(shape, array.dtype) for shape in shapes],
        [WHOLE] * len(cuts),
    )


def own_copies(units, unit, place, basis, right, sems, first):
    sectors, depth, _ = basis.shape
    slabs = lax.axis_size("slab")
    rows = depth // slabs
    copies, at = [], 0
    for start, count in units:
        for slab in range(slabs):
            copies.append(
                pltpu.make_async_copy(
                    basis.at[:, pl.ds(slab * rows, rows), pl.ds(first_column(start, place, unit), count * unit)],
                    right.at[pl.ds(0, sectors), slab % 2, slab // 2, :, pl.ds(at, count * unit)],
                    sems.at[first + len(copies)],
                )
            )
        at += count * unit
    return copies


def next_copies(nexts, place, arrays, side, right, sems, first):
    sectors = right.shape[0] // 2
    copies = []
    for array, runs in zip(arrays, nexts):
        index = 0
        for sector, slab, count, column in runs:
            copies.append(
                pltpu.make_async_copy(
                    array.at[pl.ds(index, count)],
                    right.at[
                        sectors + sector, (place[0] + side) % 2, pl.ds(slab, count), :, pl.ds(column, array.shape[2])
                    ],
                    sems.at[first + len(copies)],
                )
            )
            index += count
    return copies


def half_copy(half, distance, place, left, sem):
    slabs = lax.axis_size("slab")
    width = half.shape[3]
    slab = place[0] ^ distance
    column = pl.multiple_of(((slab % 2) * (slabs // 2) + slab // 2) * width, width)
    return pltpu.make_async_copy(half, left.at[:, :, :, pl.ds(column, width)], sem)


def gather_kernel(groups, nexts, unit, distances, cuts, place, basis, *refs):
    halves, refs = refs[: len(distances)], refs[len(distances) :]
    pairs, refs = [refs[2 * i : 2 * i + 2] for i in range(len(nexts))], refs[2 * len(nexts) :]
    left, *rights, sent, sems = refs
    copies = next_copies(nexts, place, [pair[0] for pair in pairs], 0, rights[0], sems, 0)
    copies += next_copies(nexts, place, [pair[1] for pair in pairs], 1, rights[0], sems, len(copies))
    for units, right in zip(groups, rights):
        copies += own_copies(units, unit, place, basis, right, sems, len(copies))
    for half, distance in zip(halves, distances):
        copies.append(half_copy(half, distance, place, left, sems.at[len(copies)]))
    for at, cut in enumerate(cuts):
        copies.append(pltpu.make_async_copy(pairs[-1][0].at[cut], sent.at[at], sems.at[len(copies)]))
    run(copies)


def gather(basis, groups, nexts, unit, pairs, halves, distances, cuts):
    sectors, depth, _ = basis.shape
    flavours, width = halves[0].shape[1:3]
    given = [in_vmem(array) for array in (basis, *halves, *(array for pair in pairs for array in pair))]
    copies = sum(map(len, groups)) * (depth // width) + 2 * sum(len(holds) for holds in nexts)
    shapes = [pltpu.VMEM((sectors, flavours, width, depth), jnp.bfloat16)]
    for units in groups:
        columns = sum(count for _, count in units) * unit
        shapes.append(pltpu.VMEM((2 * sectors, 2, depth // width // 2, width, columns), jnp.bfloat16))
    shapes.append(pltpu.VMEM((len(cuts), width, unit), jnp.bfloat16))
    return kernel_call(
        functools.partial(gather_kernel, groups, nexts, unit, distances, cuts),
        "gather",
        basis.shape[:2],
        given,
        [WHOLE] * len(given),
        shapes,
        [WHOLE] * len(shapes),
        [pltpu.SemaphoreType.DMA((copies + len(halves) + len(cuts),))],
    )


def product(place, partner, sector, flavour, left, right):
    index = (partner[...][sector, flavour] - place[1] + place[2]) % place[2]
    rows = right[index].reshape(left.shape[3], right.shape[4])
    return jnp.dot(left[sector, flavour], rows, preferred_element_type=jnp.float32).astype(jnp.bfloat16)


def early_kernel(distance, place, partner, half, right, _, left, stage, sem):
    run([half_copy(half, distance, place, left, sem)])
    sectors, flavours = left.shape[:2]
    for sector in range(sectors):
        for flavour in range(flavours):
            stage[flavour, sector] = product(place, partner, sector, flavour, left, right)


def early_products(partner, half, distance, left, right):
    sectors, flavours, width, _ = left.shape
    return kernel_call(
        functools.partial(early_kernel, distance),
        "early",
        (left.shape[0], left.shape[3]),
        [partner, in_vmem(half), in_vmem(right), in_vmem(left)],
        [WHOLE] + [WHOLE] * 3,
        [
            pltpu.VMEM(left.shape, left.dtype),
            pltpu.VMEM((flavours, sectors, width, right.shape[4]), jnp.bfloat16),
        ],
        [WHOLE] * 2,
        [pltpu.SemaphoreType.DMA],
        {3: 0},
    )


def partial(place, partner, sector, flavour, side, left, right):
    index = (partner[...][sector, flavour] - place[1] + place[2]) % place[2]
    core = (place[0] + side) % 2
    half = left.shape[3] // 2
    rows = right[index, core].reshape(half, right.shape[4])
    columns = pl.ds(pl.multiple_of(core * half, half), half)
    return jnp.dot(left[sector, flavour, :, columns], rows, preferred_element_type=jnp.float32)


def own_rows_kernel(groups, place, partner, left, *refs):
    arrays = []
    for nexts in groups:
        arrays.append(refs[: len(nexts)])
        refs = refs[len(nexts) :]
    refs = refs[len(groups) :]
    totals, rights, sems = refs[: len(groups)], refs[len(groups) : 2 * len(groups)], refs[2 * len(groups) :]
    copies = [
        next_copies(nexts, place, here, 0, right, sem, 0)
        for nexts, here, right, sem in zip(groups, arrays, rights, sems)
    ]
    for group in copies:
        for copy in group:
            copy.start()
    sectors, flavours = left.shape[:2]
    for group, total, right in zip(copies, totals, rights):
        for copy in group:
            copy.wait()
        for sector in range(sectors):
            for flavour in range(flavours):
                total[flavour, sector] = partial(place, partner, sector, flavour, 0, left, right)


def own_rows(partner, groups, arrays, left, rights):
    sectors, flavours, width, depth = left.shape
    given = [in_vmem(array) for array in (left, *(array for group in arrays for array in group), *rights)]
    first = 1 + len(given) - len(rights)
    return kernel_call(
        functools.partial(own_rows_kernel, groups),
        "own_rows",
        (sectors, depth),
        [partner, *given],
        [WHOLE] * (1 + len(given)),
        [pltpu.VMEM((flavours, sectors, width, right.shape[4]), jnp.float32) for right in rights]
        + [pltpu.VMEM(right.shape, right.dtype) for right in rights],
        [WHOLE] * (2 * len(rights)),
        [pltpu.SemaphoreType.DMA((sum(map(len, nexts)),)) for nexts in groups],
        {first + at: len(rights) + at for at in range(len(rights))},
    )


def late_kernel(earlier_units, units, nexts, unit, place, partner, left, total, *refs):
    earlier, refs = refs[: len(earlier_units)], refs[len(earlier_units) :]
    arrays, (_, out, right, stage, sems, early_sems, out_sems) = refs[: len(nexts)], refs[len(nexts) :]
    sectors, flavours = left.shape[:2]
    next_here = next_copies(nexts, place, arrays, 1, right, sems, 0)
    for copy in next_here:
        copy.start()
    out_copies = []
    for result, spans in zip(earlier, earlier_units):
        at = 0
        for start, count in spans:
            out_copies.append(
                pltpu.make_async_copy(
                    result.at[:, :, :, pl.ds(at, count * unit)],
                    out.at[:, :, :, pl.ds(first_column(start, place, unit), count * unit)],
                    early_sems.at[len(out_copies)],
                )
            )
            out_copies[-1].start()
            at += count * unit
    for copy in next_here:
        copy.wait()
    for sector in range(sectors):
        for flavour in range(flavours):
            rest = partial(place, partner, sector, flavour, 1, left, right)
            stage[flavour, sector] = (total[flavour, sector] + rest).astype(jnp.bfloat16)
        at = 0
        for number, (start, count) in enumerate(units):
            copy = pltpu.make_async_copy(
                stage.at[:, sector, :, pl.ds(at, count * unit)],
                out.at[:, sector, :, pl.ds(first_column(start, place, unit), count * unit)],
                out_sems.at[sector * flavours, number],
            )
            copy.start()
            out_copies.append(copy)
            at += count * unit
    for copy in out_copies:
        copy.wait()


def late_products(partner, groups, nexts, unit, arrays, left, total, earlier, right):
    sectors, flavours, width, depth = left.shape
    given = [in_vmem(array) for array in (left, total, *earlier, *arrays, right)]
    return kernel_call(
        functools.partial(late_kernel, groups[:-1], groups[-1], nexts, unit),
        "late",
        (sectors, depth),
        [partner, *given],
        [WHOLE] * (1 + len(given)),
        [
            pltpu.HBM((flavours, sectors, width, depth), jnp.bfloat16),
            pltpu.VMEM(right.shape, right.dtype),
        ],
        [ANY, WHOLE],
        [
            pltpu.VMEM((flavours, sectors, width, right.shape[4]), jnp.bfloat16),
            pltpu.SemaphoreType.DMA((sum(map(len, nexts)),)),
            pltpu.SemaphoreType.DMA((sum(map(len, groups[:-1])),)),
            pltpu.SemaphoreType.DMA((sectors * flavours, len(groups[-1]))),
        ],
        {len(given): 1},
    )[0]


def local(basis, fermion, partner):
    sectors, depth, _ = basis.shape
    unit = depth // 8
    partner = partner.T
    distances = tuple(reversed(range(lax.axis_size("slab"))))
    slabs = range(lax.axis_size("slab") // 2)
    held = [(sector, slab) for sector in range(sectors) for slab in slabs]
    alone = len(held) // 4
    count = 3
    units = ((0, count), (OWN, 1)), ((count, 6 - count), (OTHER, 1))
    first_blocks = [(sector, units[0], slab) for sector, slab in held]
    last_blocks = [(sector, ((start, 1),), slab) for start in range(count, 6) for sector, slab in held]
    last_blocks += [(sector, ((OTHER, 1),), slab) for sector, slab in held[:alone]]
    first_part, *far = basis_part(basis, fermion, first_blocks, unit, distances[:2])
    first = previous(first_part)
    far3, far2 = far_blocks(basis, fermion, distances[:2], far)
    got3, got2 = swapped(far3, distances[0]), swapped(far2, distances[1])
    mine, near, last_part = near_blocks(basis, fermion, last_blocks, unit, distances[2:], far2)
    beside, last = swapped(mine, distances[2]), previous(last_part)

    def runs(column, blocks):
        found = []
        for sector, slab in blocks:
            if found and found[-1][0] == sector:
                found[-1][2] += 1
            else:
                found.append([sector, slab, 1, column])
        return found

    groups = ((0, 2), (2, 4))
    every = slice(None)
    pieces = cut_out(first, [(every, every, slice(begin * unit, end * unit)) for begin, end in groups], (beside, got2))
    pairs = [(piece, swapped(piece, 1)) for piece in pieces]
    nexts = [runs(begin * unit, held) for begin, _ in groups]
    cuts = [(at, every, pl.ds((groups[-1][1] - groups[-1][0] - 1) * unit, unit)) for at in range(alone, len(held))]
    left, early_right, late_right, sent = gather(
        basis, units, nexts, unit, pairs, [got2, beside, near], distances[1:], cuts
    )
    other = swapped(sent, distances[1])
    left, early = early_products(partner, got3, distances[0], left, early_right)
    last, other, early = lax.optimization_barrier((last, other, early))
    last_other, other_other = swapped(last, 1), swapped(other, 1)
    nexts = [[], runs((6 - count) * unit, held[alone:])]
    for at in range(6 - count):
        nexts[0] += runs(at * unit, held)
    nexts[0] += runs((6 - count) * unit, held[:alone])
    total, late_right = own_rows(partner, [nexts], [[last, other]], left, [late_right])
    return late_products(
        partner, units, nexts, unit, [last_other, other_other], left, total, [early], late_right
    )


def solution(mesh):
    placed = (P("sec", None, None), P(None, "sec", None, "slab"), P(None, "sec"))
    return jax.shard_map(
        local, mesh=mesh, in_specs=placed, out_specs=P(None, "sec", "slab", None), check_vma=False
    )
```
